32 devices in a mesh: aper: 8 (over y, x, core), shot: 4 (over z).
Axes of the slice: x: 2, y: 2, z: 4, core: 2. Of those that a mesh axis runs over, the one named last changes fastest.
Arguments:
- wavefield: float32 [4, 9, 32, 128, 128], P('shot', None, 'aper'), may hold values from -6 to 6
- lame_lambda: float32 [32, 128, 128], P('aper', 'shot'), may hold values from 0.5 to 2
- lame_mu: float32 [32, 128, 128], P('aper', 'shot'), may hold values from 0.3 to 1
- buoyancy: float32 [32, 128, 128], P('aper', 'shot'), may hold values from 0.4 to 1
- quality: float32 [32, 128, 128], P('aper', 'shot'), may hold values from 0.05 to 2
- active: int32 [4, 8, 4, 4], replicated, may hold values 0 or 1
Outputs:
- final_field: float32 [4, 9, 32, 128, 128], P('shot', None, 'aper')
The draws below stay inside these ranges and needn't reach their ends.
All inputs are finite; a program needn't handle non-finite values.
Results may differ from the reference program's by a relative error of at most 0.00002.
Values sent between devices are 32-bit elements; how exact they have to be, the bound alone decides.
No kernel may reach another device: no remote copies, remote signals or barrier semaphores. Data moves between devices by JAX's collectives and lax.ppermute only.
A program may use at most 64 MiB of HBM per device.

```python
import math
import jax
import jax.numpy as jnp
from jax import lax

CX = 4
NY = 128
NZ = 128
BLK = 32
STEPS = 4
SHOTS = 4
NX = 32
NBY = 4
NBZ = 4
N_APER = 8


def with_ends(array, key, smallest, largest):
    longest = array.shape.index(max(array.shape))
    spots = []
    for shift in (0, 1):
        where = [jax.random.randint(jax.random.fold_in(key, axis), (), 0, length) for axis, length in enumerate(array.shape)]
        where[longest] = (where[longest] + shift) % array.shape[longest]
        spots.append(tuple(where))
    return array.at[spots[0]].set(smallest).at[spots[1]].set(largest)


def block_scale(rng, extent, pieces, least, largest):
    level, own = 1.0, jax.random.fold_in(rng, 6)
    for axis_at, blocks in pieces:
        draws = jnp.exp(jax.random.uniform(jax.random.fold_in(own, axis_at), (blocks,), jnp.float32, least / len(pieces), largest / len(pieces)))
        level = level * jnp.repeat(draws, extent[axis_at] // blocks).reshape([-1 if axis == axis_at else 1 for axis in range(len(extent))])
    return level


def normal_values(key, dims, scale, reach, shards=(), held_as=jnp.bfloat16):
    entries = scale * jax.random.normal(key, dims, jnp.float32)
    if shards:
        entries = entries * block_scale(key, dims, shards, -0.22, 0.18)
    return jnp.clip(entries, -reach, reach).astype(held_as)


def setup_inputs(seed: int = 0) -> dict:
    streams_of = jax.random.split(jax.random.key(seed), 7)
    wavefield = normal_values(streams_of[0], (SHOTS, 9, NX, NY, NZ), 1.0, 6.0, ((0, 4), (2, 8)), jnp.float32)
    lame_lambda = jnp.clip(jnp.exp(math.log(2.0) - 1.3862944 * jax.random.uniform(streams_of[1], (NX, NY, NZ), jnp.float32) ** block_scale(streams_of[1], (NX, NY, NZ), ((0, 8), (1, 4)), -0.2, 0.2)), 0.5, 2.0)
    lame_mu = jnp.clip(jnp.exp(math.log(1.0) - 1.2039728 * jax.random.uniform(streams_of[2], (NX, NY, NZ), jnp.float32) ** block_scale(streams_of[2], (NX, NY, NZ), ((0, 8), (1, 4)), -0.2, 0.2)), 0.3, 1.0)
    buoyancy = jnp.clip(jnp.exp(math.log(1.0) - 0.9162907 * jax.random.uniform(streams_of[3], (NX, NY, NZ), jnp.float32) ** block_scale(streams_of[3], (NX, NY, NZ), ((0, 8), (1, 4)), -0.2, 0.2)), 0.4, 1.0)
    quality = jnp.clip(jnp.exp(math.log(2.0) - 3.6888794 * jax.random.uniform(streams_of[4], (NX, NY, NZ), jnp.float32) ** block_scale(streams_of[4], (NX, NY, NZ), ((0, 8), (1, 4)), -0.2, 0.2)), 0.05, 2.0)
    active = with_ends((jax.random.randint(streams_of[5], (STEPS, N_APER, NBY, NBZ), 0, 4) < 3).astype(jnp.int32), jax.random.fold_in(streams_of[5], 1), 0, 1)
    return dict(wavefield=wavefield, lame_lambda=lame_lambda, lame_mu=lame_mu, buoyancy=buoyancy, quality=quality, active=active)


COEF_NEAR = 1.125
COEF_FAR = -1.0 / 24.0
TIME_STEP = 0.2


def forward_rows(values, offset, length):
    return COEF_NEAR * (values[offset + 1:offset + 1 + length] - values[offset:offset + length]) + COEF_FAR * (values[offset + 2:offset + 2 + length] - values[offset - 1:offset - 1 + length])


def backward_rows(values, offset, length):
    return COEF_NEAR * (values[offset:offset + length] - values[offset - 1:offset - 1 + length]) + COEF_FAR * (values[offset + 1:offset + 1 + length] - values[offset - 2:offset - 2 + length])


def shifted(values, along, amount):
    widths = [(0, 0)] * values.ndim
    widths[along] = (2, 2)
    padded = jnp.pad(values, widths)
    return lax.slice_in_dim(padded, 2 + amount, 2 + amount + values.shape[along], axis=along)


def forward_axis(values, along):
    return COEF_NEAR * (shifted(values, along, 1) - values) + COEF_FAR * (shifted(values, along, 2) - shifted(values, along, -1))


def backward_axis(values, along):
    return COEF_NEAR * (values - shifted(values, along, -1)) + COEF_FAR * (shifted(values, along, 1) - shifted(values, along, -2))


def velocity_update(previous, stress, offset, length, buoyancy, damping, active_cells):
    def pick_rows(values):
        return values[offset:offset + length]
    grad_first = forward_rows(stress[0], offset, length) + backward_axis(pick_rows(stress[3]), 1) + backward_axis(pick_rows(stress[4]), 2)
    grad_second = backward_rows(stress[3], offset, length) + forward_axis(pick_rows(stress[1]), 1) + backward_axis(pick_rows(stress[5]), 2)
    grad_third = backward_rows(stress[4], offset, length) + backward_axis(pick_rows(stress[5]), 1) + forward_axis(pick_rows(stress[2]), 2)
    forcing = jnp.stack([grad_first, grad_second, grad_third])
    return previous + active_cells * (damping * (previous + TIME_STEP * buoyancy * forcing) - previous)


def stress_update(previous, velocity, offset, length, lambda_field, shear, damping, active_cells):
    def pick_rows(values):
        return values[offset:offset + length]
    strain_first = backward_rows(velocity[0], offset, length)
    strain_second = backward_axis(pick_rows(velocity[1]), 1)
    strain_third = backward_axis(pick_rows(velocity[2]), 2)
    dilation = strain_first + strain_second + strain_third
    shear_xy = forward_axis(pick_rows(velocity[0]), 1) + forward_rows(velocity[1], offset, length)
    shear_xz = forward_axis(pick_rows(velocity[0]), 2) + forward_rows(velocity[2], offset, length)
    shear_yz = forward_axis(pick_rows(velocity[1]), 2) + forward_axis(pick_rows(velocity[2]), 1)
    rates = jnp.stack([lambda_field * dilation + 2.0 * shear * strain_first, lambda_field * dilation + 2.0 * shear * strain_second, lambda_field * dilation + 2.0 * shear * strain_third, shear * shear_xy, shear * shear_xz, shear * shear_yz])
    return previous + active_cells * (damping * (previous + TIME_STEP * rates) - previous)


def reference(wavefield, lame_lambda, lame_mu, buoyancy, quality, active):
    damping = jnp.exp(-TIME_STEP * quality)
    length = lame_lambda.shape[0]
    rim_widths = ((0, 0), (2, 2), (0, 0), (0, 0))
    masks = []
    for moment in range(STEPS):
        blocks = active[moment].astype(jnp.float32)
        blocks = jnp.repeat(jnp.repeat(jnp.repeat(blocks, CX, axis=0), BLK, axis=1), BLK, axis=2)
        masks.append(blocks)

    def advance(values):
        for moment in range(STEPS):
            stress_pad = jnp.pad(values[3:], rim_widths)
            velocity = velocity_update(values[:3], stress_pad, 2, length, buoyancy, damping, masks[moment])
            velocity_pad = jnp.pad(velocity, rim_widths)
            stress = stress_update(values[3:], velocity_pad, 2, length, lame_lambda, lame_mu, damping, masks[moment])
            values = jnp.concatenate([velocity, stress], axis=0)
        return values

    return lax.map(advance, wavefield)
```

```python
import functools

import jax
import jax.numpy as jnp
from jax import lax
from jax.experimental import pallas as pl
from jax.experimental.pallas import tpu as pltpu
from jax.sharding import PartitionSpec as P

NEAR = 1.125
FAR = -1.0 / 24.0
DT = 0.2
ROWS = 8
PAD = 8
REACH = 3
VMEM = pl.BlockSpec(memory_space=pltpu.VMEM)
ANY = pl.BlockSpec(memory_space=pl.ANY)
F32 = jnp.float32


def call(body, ins, outs, alias=(), scratch=(), anywhere=(), flops=1_000_000):
    in_names, out_names = list(ins), list(outs)

    def kernel(*refs):
        names = {}
        for name, ref in zip(in_names, refs):
            if name not in alias:
                names[name] = ref
        for name, ref in zip(out_names, refs[len(in_names):]):
            names[name] = ref
        body(names, *refs[len(in_names) + len(out_names):])

    size = sum(4 * a.size for a in ins.values())
    ins = {name: pltpu.with_memory_space_constraint(a, pltpu.HBM) if name in anywhere
           else pltpu.with_memory_space_constraint(a, pltpu.VMEM) if name in alias
           else a for name, a in ins.items()}
    results = pl.pallas_call(
        kernel,
        out_shape=[pltpu.HBM(shape, F32) if name in anywhere else pltpu.VMEM(shape, F32)
                   for name, shape in outs.items()],
        in_specs=[ANY if name in anywhere else VMEM for name in in_names],
        out_specs=[ANY if name in anywhere else VMEM for name in out_names],
        scratch_shapes=list(scratch),
        input_output_aliases={in_names.index(n): out_names.index(n) for n in alias},
        compiler_params=pltpu.CompilerParams(vmem_limit_bytes=24 * 2**20),
        cost_estimate=pl.CostEstimate(flops=flops, bytes_accessed=size, transcendentals=0),
    )(*ins.values())
    return dict(zip(out_names, results))


def odd_slab():
    return lax.rem(lax.axis_index("aper"), 2) == 1


def pick(flag, yes, no):
    return jnp.where(flag, jnp.int32(yes), jnp.int32(no))


class Shifts:
    def __init__(self, lanes):
        lane = lax.broadcasted_iota(jnp.int32, (ROWS, lanes), 1)
        self.lanes = lanes
        self.f_up1 = jnp.where(lane < lanes - 1, F32(NEAR), F32(0))
        self.f_up2 = jnp.where(lane < lanes - 2, F32(FAR), F32(0))
        self.f_dn1 = jnp.where(lane >= 1, F32(-FAR), F32(0))
        self.b_dn1 = jnp.where(lane >= 1, F32(-NEAR), F32(0))
        self.b_dn2 = jnp.where(lane >= 2, F32(-FAR), F32(0))
        self.b_up1 = jnp.where(lane < lanes - 1, F32(FAR), F32(0))

    def fz(self, f):
        n = self.lanes
        return (self.f_up1 * pltpu.roll(f, n - 1, 1) - NEAR * f) + (
            self.f_up2 * pltpu.roll(f, n - 2, 1) + self.f_dn1 * pltpu.roll(f, 1, 1)
        )

    def bz(self, f):
        n = self.lanes
        return (self.b_dn1 * pltpu.roll(f, 1, 1) + NEAR * f) + (
            self.b_up1 * pltpu.roll(f, n - 1, 1) + self.b_dn2 * pltpu.roll(f, 2, 1)
        )


def fwd(at):
    return NEAR * (at(1) - at(0)) + FAR * (at(2) - at(-1))


def bwd(at):
    return NEAR * (at(0) - at(-1)) + FAR * (at(1) - at(-2))


def tile_reader(ref, field, start):
    seen = {}

    def read(layer, dy=0):
        if (layer, dy) not in seen:
            seen[layer, dy] = ref[field, layer, pl.ds(start + PAD + dy, ROWS), :]
        return seen[layer, dy]

    return read


def factors(active_cells, damp):
    return jnp.where(active_cells, damp, F32(1)), jnp.where(active_cells, DT * damp, F32(0))


def mask_rows(refs, moment, slab, start, blocks, block_rows):
    row = (moment * 3 + slab) * blocks + start // block_rows
    return jnp.broadcast_to(refs["mask"][pl.ds(row, 1), :], (ROWS, refs["mask"].shape[1])) > 0


def zero_pads(ref, rows):
    zeros = jnp.zeros((ref.shape[0], ref.shape[1], PAD, ref.shape[3]), F32)
    ref[:, :, :PAD, :] = zeros
    ref[:, :, PAD + rows:, :] = zeros


class Plan:
    def __init__(self, cx, rows, lanes, blocks, steps, cuts):
        self.cx, self.rows, self.lanes = cx, rows, lanes
        self.blocks, self.steps, self.cuts = blocks, steps, cuts
        self.block_rows = rows // blocks
        self.tiles = rows // ROWS

    def chunk(self, step, which):
        cut = self.cuts[step]
        return (0, cut) if which == 0 else (cut, self.tiles)

    def slots(self, step):
        n = self.cx
        if step < self.steps - 1:
            return [
                ((f, n + j), (f, REACH + j), (f, j), (f, n + REACH + j))
                for f in range(3) for j in range(REACH)
            ]
        top = [(0, n + 1), (0, n + 2), (1, n + 2), (2, n + 2), (2, n + 2)]
        bottom = [(0, 3), (1, 4), (1, 3), (2, 3), (2, 4)]
        below = [(0, 1), (0, 2), (1, 2), (2, 2), (2, 2)]
        above = [(0, n + 3), (1, n + 4), (1, n + 3), (2, n + 3), (2, n + 4)]
        return list(zip(top, bottom, below, above))

    def velocity(self, refs, moment, which, sh, so, previous):
        first, last = self.chunk(moment, which)
        z = Shifts(self.lanes)

        def tile(k, carry):
            start = pl.multiple_of(k * ROWS, ROWS)
            here = mask_rows(refs, moment, 1, start, self.blocks, self.block_rows)
            xx = tile_reader(sh, 0, start)
            xy = tile_reader(sh, 1, start)
            xz = tile_reader(sh, 2, start)
            yy = tile_reader(so, 0, start)
            zz = tile_reader(so, 1, start)
            yz = tile_reader(so, 2, start)
            for i in range(self.cx):
                keep, gain = factors(here, refs["damp"][i, pl.ds(start, ROWS), :])
                gain = gain * refs["buoy"][i, pl.ds(start, ROWS), :]
                gx = fwd(lambda d: xx(i + 1 + d)) + bwd(lambda d: xy(i + 2, d)) + z.bz(xz(i + 2))
                gy = bwd(lambda d: xy(i + 2 + d)) + fwd(lambda d: yy(i, d)) + z.bz(yz(i))
                gz = bwd(lambda d: xz(i + 2 + d)) + bwd(lambda d: yz(i, d)) + z.fz(zz(i))
                for f, g in enumerate((gx, gy, gz)):
                    refs["vel_next"][f, REACH + i, pl.ds(start + PAD, ROWS), :] = (
                        keep * previous(f, i, start) + gain * g
                    )
            return carry

        lax.fori_loop(first, last, tile, 0)
        odd = odd_slab()
        rows = pl.ds(PAD + first * ROWS, (last - first) * ROWS)
        for slot, (top, bottom, _, _) in enumerate(self.slots(moment)):
            field, layer = pick(odd, top[0], bottom[0]), pick(odd, top[1], bottom[1])
            refs["send_far"][slot] = refs["vel_next"][field, layer, rows, :]
            field, layer = pick(odd, bottom[0], top[0]), pick(odd, bottom[1], top[1])
            refs["send_near"][slot] = refs["vel_next"][field, layer, rows, :]

    def arrivals(self, refs, moment, which):
        first, last = self.chunk(moment, which)
        odd = odd_slab()
        rows = pl.ds(PAD + first * ROWS, (last - first) * ROWS)
        for slot, (_, _, below, above) in enumerate(self.slots(moment)):
            field, layer = pick(odd, above[0], below[0]), pick(odd, above[1], below[1])
            refs["vel"][field, layer, rows, :] = refs["from_far"][slot]
            field, layer = pick(odd, below[0], above[0]), pick(odd, below[1], above[1])
            refs["vel"][field, layer, rows, :] = refs["from_near"][slot]

    def stress_tiles(self, moment, which):
        first, last = self.chunk(moment, which)
        if which == 1:
            return first - 1, last
        return first, last - 1 if moment == self.steps - 1 else last

    def stress(self, refs, moment, which, final, part=None):
        first, last = part or self.stress_tiles(moment, which)
        base = self.stress_tiles(moment, which)[0]
        n = self.cx
        z = Shifts(self.lanes)
        old_h, old_o = refs["sh"], refs["so"]

        def tile(k, carry):
            start = pl.multiple_of(k * ROWS, ROWS)
            masks = [mask_rows(refs, moment, slab, start, self.blocks, self.block_rows) for slab in range(3)]
            vx = tile_reader(refs["vel"], 0, start)
            vy = tile_reader(refs["vel"], 1, start)
            vz = tile_reader(refs["vel"], 2, start)
            rows = pl.ds(start, ROWS)
            padded = pl.ds(start + PAD, ROWS)

            def put_h(field, i, value):
                if final:
                    refs["done"][(0, 3, 4)[field], i, pl.ds(start - base * ROWS, ROWS), :] = value
                else:
                    refs["sh_next"][field, i + (1, 2, 2)[field], padded, :] = value

            def put_o(field, i, value):
                if final:
                    refs["done"][(1, 2, 5)[field], i, pl.ds(start - base * ROWS, ROWS), :] = value
                else:
                    refs["so_next"][field, i, padded, :] = value

            for i in range(0, n) if final else range(-2, n + 2):
                own = 0 <= i < n
                if own:
                    damp = refs["damp"][i, rows, :]
                else:
                    damp = refs["damp_edge"][i + 2 if i < 0 else i - n + 2, rows, :]
                keep, gain = factors(masks[0 if i < 0 else 1 if own else 2], damp)
                at = i + REACH
                mu = gain * refs["mu"][i + 2, rows, :]
                if i >= -1:
                    ex = bwd(lambda d: vx(at + d))
                    ey = bwd(lambda d: vy(at, d))
                    ez = z.bz(vz(at))
                    spread = gain * refs["lam"][i + 1, rows, :] * (ex + ey + ez)
                    mu2 = mu + mu
                    put_h(0, i, keep * old_h[0, i + 1, padded, :] + (spread + mu2 * ex))
                if own:
                    put_o(0, i, keep * old_o[0, i, padded, :] + (spread + mu2 * ey))
                    put_o(1, i, keep * old_o[1, i, padded, :] + (spread + mu2 * ez))
                    yz = z.fz(vy(at)) + fwd(lambda d: vz(at, d))
                    put_o(2, i, keep * old_o[2, i, padded, :] + mu * yz)
                if i <= n:
                    xy = fwd(lambda d: vx(at, d)) + fwd(lambda d: vy(at + d))
                    put_h(1, i, keep * old_h[1, i + 2, padded, :] + mu * xy)
                    xz = z.fz(vx(at)) + fwd(lambda d: vz(at + d))
                    put_h(2, i, keep * old_h[2, i + 2, padded, :] + mu * xz)
            return carry

        lax.fori_loop(first, last, tile, 0)

    def finish(self, refs, moment, which, done, sems):
        refs = dict(refs, done=done)
        first, last = self.stress_tiles(moment, which)
        copies = []

        def move(src, dst):
            copy = pltpu.make_async_copy(src, dst, sems.at[len(copies)])
            copy.start()
            copies.append(copy)

        for f in range(3):
            span = (last - first) * ROWS
            move(refs["vel"].at[f, pl.ds(REACH, self.cx), pl.ds(PAD + first * ROWS, span)],
                 refs["out"].at[0, f, :, pl.ds(first * ROWS, span)])
        for a, b in self.parts(first, last):
            self.stress(refs, moment, which, True, (a, b))
            span = (b - a) * ROWS
            for f in range(6):
                move(done.at[f, :, pl.ds((a - first) * ROWS, span)],
                     refs["out"].at[0, 3 + f, :, pl.ds(a * ROWS, span)])
        for copy in copies:
            copy.wait()

    @staticmethod
    def parts(first, last):
        middle = (first + last + 1) // 2
        return [(a, b) for a, b in ((first, middle), (middle, last)) if b > a]


STRESS_SLOTS = 5
MODEL_SLOTS = 6


def pack(cx, panel_rows, rows, refs, sems):
    odd = odd_slab()
    copies = []

    def move(src, dst):
        copy = pltpu.make_async_copy(src, dst, sems.at[len(copies)])
        copy.start()
        copies.append(copy)

    top = [(3, cx - 1), (6, cx - 2), (6, cx - 1), (7, cx - 2), (7, cx - 1)]
    bottom = [(3, 0), (3, 1), (6, 0), (7, 0), (7, 0)]
    for name, flag in (("far", odd), ("near", jnp.logical_not(odd))):
        for slot in range(STRESS_SLOTS):
            field = pick(flag, top[slot][0], bottom[slot][0])
            layer = pick(flag, top[slot][1], bottom[slot][1])
            move(refs["wave"].at[0, field, layer], refs[name].at[pl.ds(slot * rows, rows)])
        base = STRESS_SLOTS * rows
        for slot in range(MODEL_SLOTS):
            array = refs[("lam", "lam", "mu", "mu", "q", "q")[slot]]
            layer = pick(flag, cx - 2 + slot % 2, slot % 2)
            move(array.at[layer], refs[name].at[pl.ds(base + slot * panel_rows, panel_rows)])
    for i, name in enumerate(("buoy", "q")):
        move(refs[name], refs["first"].at[pl.ds(i * cx, cx)])
    for i, name in enumerate(("lam", "mu")):
        move(refs[name], refs["second"].at[pl.ds(i * cx, cx)])
    for copy in copies:
        copy.wait()


def prepare(cx, rows, refs):
    zero_pads(refs["sh"], rows)
    zero_pads(refs["so"], rows)
    inner = pl.ds(PAD, rows)
    for field, (source, shift) in enumerate(((3, 1), (6, 2), (7, 2))):
        for i in range(cx):
            refs["sh"][field, i + shift, inner, :] = refs["wave"][0, source, i]
    for field, source in enumerate((4, 5, 8)):
        for i in range(cx):
            refs["so"][field, i, inner, :] = refs["wave"][0, source, i]
    for field in range(3):
        for i in range(cx):
            refs["old"][field, i] = refs["wave"][0, field, i]


def panel_place(k, shots, panel_rows):
    return pl.ds(pl.multiple_of(partner(lax.axis_index("shot"), k, shots) * panel_rows, panel_rows), panel_rows)


def partner(index, k, shots):
    if shots & (shots - 1) == 0:
        return index ^ k
    return lax.rem(index + shots - k, shots)


def panel_pairs(k, shots):
    if shots & (shots - 1) == 0:
        return [(i, i ^ k) for i in range(shots)]
    return [(i, (i + k) % shots) for i in range(shots)]


def per_device(cuts_of, shots, slabs, wave, lam, mu, buoy, q, active):
    cx, panel_rows, lanes = lam.shape
    rows = wave.shape[3]
    steps, _, blocks, lane_blocks = active.shape
    plan = Plan(cx, rows, lanes, blocks, steps, cuts_of(steps, rows // ROWS))
    padded = rows + 2 * PAD
    far = [(i, i + 1) for i in range(1, slabs - 1, 2)]
    near = [(i, i + 1) for i in range(0, slabs - 1, 2)]
    far = far + [(j, i) for i, j in far]
    near = near + [(j, i) for i, j in near]

    def exchange(to_far, to_near):
        return lax.ppermute(to_far, "aper", far), lax.ppermute(to_near, "aper", near)

    def gather(mine):
        return [mine] + [lax.ppermute(mine, "shot", panel_pairs(k, shots)) for k in range(1, shots)]

    halo_rows = STRESS_SLOTS * rows + MODEL_SLOTS * panel_rows
    sent = call(
        functools.partial(pack, cx, panel_rows, rows),
        dict(wave=wave, lam=lam, mu=mu, buoy=buoy, q=q),
        dict(far=(halo_rows, lanes), near=(halo_rows, lanes),
             first=(2 * cx, panel_rows, lanes), second=(2 * cx, panel_rows, lanes)),
        scratch=[pltpu.SemaphoreType.DMA((2 * (STRESS_SLOTS + MODEL_SLOTS) + 4,))],
        anywhere=("wave", "lam", "mu", "buoy", "q"),
    )
    halo_far, halo_near = exchange(sent["far"], sent["near"])
    firsts = gather(sent["first"])
    seconds = gather(sent["second"])
    edge = jnp.concatenate([halo_far[STRESS_SLOTS * rows:], halo_near[STRESS_SLOTS * rows:]])
    edges = gather(edge)

    device = lax.axis_index("aper")
    around = lax.dynamic_slice_in_dim(jnp.pad(active, ((0, 0), (1, 1), (0, 0), (0, 0))), device, 3, 1)
    mask = jnp.repeat(around.astype(F32).reshape(steps * 3 * blocks, lane_blocks), lanes // lane_blocks, axis=1)

    sh_shape, so_shape = (3, cx + 3, padded, lanes), (3, cx, padded, lanes)
    vel_shape, slab_shape = (3, cx + 2 * REACH, padded, lanes), (cx, rows, lanes)
    state = call(functools.partial(prepare, cx, rows), dict(wave=wave),
                 dict(sh=sh_shape, so=so_shape, old=(3,) + slab_shape))

    def sends(step, which):
        first, last = plan.chunk(step, which)
        shape = (len(plan.slots(step)), (last - first) * ROWS, lanes)
        return dict(send_far=shape, send_near=shape)

    def start_first(refs):
        odd = odd_slab()
        inner = pl.ds(PAD, rows)
        below = [(0, 0), (1, 0), (1, 1), (2, 0), (2, 1)]
        above = [(0, cx + 1), (0, cx + 2), (1, cx + 2), (2, cx + 2), (2, cx + 2)]
        for slot in range(STRESS_SLOTS):
            part = pl.ds(slot * rows, rows)
            field = pick(odd, above[slot][0], below[slot][0])
            layer = pick(odd, above[slot][1], below[slot][1])
            refs["sh"][field, layer, inner, :] = refs["halo_far"][part, :]
            field = pick(odd, below[slot][0], above[slot][0])
            layer = pick(odd, below[slot][1], above[slot][1])
            refs["sh"][field, layer, inner, :] = refs["halo_near"][part, :]
        for k in range(shots):
            place = panel_place(k, shots, panel_rows)
            for i in range(cx):
                refs["buoy"][i, place, :] = refs["first%d" % k][i]
                refs["damp"][i, place, :] = jnp.exp(-DT * refs["first%d" % k][cx + i])
        zero_pads(refs["vel_next"], rows)
        start_chunk(refs, 0)

    def start_chunk(refs, which):
        plan.velocity(refs, 0, which, refs["sh"], refs["so"],
                      lambda f, i, start: refs["old"][f, i, pl.ds(start, ROWS), :])

    ins = dict(sh=state["sh"], so=state["so"], old=state["old"], mask=mask,
               halo_far=halo_far, halo_near=halo_near)
    ins.update({"first%d" % k: a for k, a in enumerate(firsts)})
    got = call(start_first, ins,
               dict(sh=sh_shape, buoy=slab_shape, damp=slab_shape, vel_next=vel_shape, **sends(0, 0)),
               alias=("sh",))
    sh, so = got["sh"], state["so"]
    model = dict(mask=mask, buoy=got["buoy"], damp=got["damp"])
    arrived = [exchange(got["send_far"], got["send_near"])]
    got = call(lambda refs: start_chunk(refs, 1),
               dict(sh=sh, so=so, old=state["old"], vel_next=got["vel_next"], **model),
               dict(vel_next=vel_shape, **sends(0, 1)), alias=("vel_next",))
    vel = got["vel_next"]
    arrived.append(exchange(got["send_far"], got["send_near"]))

    def assemble(refs):
        odd = odd_slab()
        for k in range(shots):
            place = panel_place(k, shots, panel_rows)
            for i in range(cx):
                refs["lam"][i + 1, place, :] = refs["second%d" % k][i]
                refs["mu"][i + 2, place, :] = refs["second%d" % k][cx + i]
            for half, flag in ((0, odd), (1, jnp.logical_not(odd))):
                def part(slot):
                    return refs["edge%d" % k][pl.ds((half * MODEL_SLOTS + slot) * panel_rows, panel_rows), :]
                for j in range(2):
                    layer = pick(flag, cx + 1 + j, 0)
                    if j == 1:
                        refs["lam"][layer, place, :] = part(1)
                    else:
                        refs["lam"][layer, place, :] = part(0)
                    refs["mu"][pick(flag, cx + 2 + j, j), place, :] = part(2 + j)
                    refs["damp_edge"][pick(flag, 2 + j, j), place, :] = jnp.exp(-DT * part(4 + j))

    ins = {"second%d" % k: a for k, a in enumerate(seconds)}
    ins.update({"edge%d" % k: a for k, a in enumerate(edges)})
    model.update(call(assemble, ins, dict(lam=(cx + 3, rows, lanes), mu=(cx + 4, rows, lanes),
                                          damp_edge=(4, rows, lanes))))

    out_shape = wave.shape
    for step in range(steps):
        final = step == steps - 1

        def advance(refs, *scratch, which, step=step, final=final):
            plan.arrivals(refs, step, which)
            if final:
                plan.finish(refs, step, which, *scratch)
                return
            if which == 0:
                zero_pads(refs["sh_next"], rows)
                zero_pads(refs["so_next"], rows)
                zero_pads(refs["vel_next"], rows)
            plan.stress(refs, step, which, False)
            plan.velocity(
                refs, step + 1, which, refs["sh_next"], refs["so_next"],
                lambda f, i, start: refs["vel"][f, REACH + i, pl.ds(start + PAD, ROWS), :])

        nexts = dict(out=out_shape) if final else dict(
            sh_next=sh_shape, so_next=so_shape, vel_next=vel_shape)
        following = []
        carried = {}
        for which in range(2):
            ins = dict(vel=vel, sh=sh, so=so, from_far=arrived[which][0], from_near=arrived[which][1],
                       **model, **carried)
            outs = dict(vel=vel_shape, **nexts)
            scratch = []
            if final:
                first, last = plan.stress_tiles(step, which)
                scratch = [pltpu.VMEM((6, cx, (last - first) * ROWS, lanes), F32),
                           pltpu.SemaphoreType.DMA((3 + 6 * len(plan.parts(first, last)),))]
            else:
                outs.update(sends(step + 1, which))
            got = call(functools.partial(advance, which=which), ins, outs, alias=("vel",) + tuple(carried),
                       scratch=scratch, anywhere=("out",))
            vel = got["vel"]
            carried = {name: got[name] for name in nexts}
            if not final:
                following.append(exchange(got["send_far"], got["send_near"]))
        if final:
            return carried["out"]
        vel, sh, so, arrived = carried["vel_next"], carried["sh_next"], carried["so_next"], following


def cuts_of(steps, tiles):
    middle = tiles // 2 + steps // 2
    return [max(1, middle - step) for step in range(steps)]


def solution(mesh):
    body = functools.partial(per_device, cuts_of, mesh.shape["shot"], mesh.shape["aper"])
    return jax.shard_map(
        body,
        mesh=mesh,
        in_specs=(
            P("shot", None, "aper", None, None),
            P("aper", "shot", None),
            P("aper", "shot", None),
            P("aper", "shot", None),
            P("aper", "shot", None),
            P(),
        ),
        out_specs=P("shot", None, "aper", None, None),
        check_vma=False,
    )
```

```python
import functools

import jax
import jax.numpy as jnp
from jax import lax
from jax.experimental import pallas as pl
from jax.experimental.pallas import tpu as pltpu
from jax.sharding import PartitionSpec as P

NEAR = 1.125
FAR = -1.0 / 24.0
DT = 0.2
ROWS = 8
PAD = 8
REACH = 3
VMEM = pl.BlockSpec(memory_space=pltpu.VMEM)
ANY = pl.BlockSpec(memory_space=pl.ANY)
F32 = jnp.float32


def call(body, ins, outs, alias=(), scratch=(), anywhere=(), us=0.5, waits=()):
    ins = dict(ins, **{"wait%d" % i: a for i, a in enumerate(waits)})
    in_names, out_names = list(ins), list(outs)

    def kernel(*refs):
        names = {}
        for name, ref in zip(in_names, refs):
            if name not in alias:
                names[name] = ref
        for name, ref in zip(out_names, refs[len(in_names):]):
            names[name] = ref
        body(names, *refs[len(in_names) + len(out_names):])

    ins = {name: pltpu.with_memory_space_constraint(a, pltpu.HBM) if name in anywhere
           else pltpu.with_memory_space_constraint(a, pltpu.VMEM) if name in alias
           else a for name, a in ins.items()}
    results = pl.pallas_call(
        kernel,
        out_shape=[pltpu.HBM(shape, F32) if name in anywhere else pltpu.VMEM(shape, F32)
                   for name, shape in outs.items()],
        in_specs=[ANY if name in anywhere or name[:4] == "wait" else VMEM for name in in_names],
        out_specs=[ANY if name in anywhere else VMEM for name in out_names],
        scratch_shapes=list(scratch),
        input_output_aliases={in_names.index(n): out_names.index(n) for n in alias},
        compiler_params=pltpu.CompilerParams(vmem_limit_bytes=24 * 2**20),
        cost_estimate=pl.CostEstimate(flops=int(us * 1e9), bytes_accessed=int(us * 3.6e6), transcendentals=0),
    )(*ins.values())
    return dict(zip(out_names, results))


def odd_slab():
    return lax.rem(lax.axis_index("aper"), 2) == 1


def pick(flag, yes, no):
    return jnp.where(flag, jnp.int32(yes), jnp.int32(no))


class Shifts:
    def __init__(self, lanes):
        lane = lax.broadcasted_iota(jnp.int32, (ROWS, lanes), 1)
        self.lanes = lanes
        self.f_up1 = jnp.where(lane < lanes - 1, F32(NEAR), F32(0))
        self.f_up2 = jnp.where(lane < lanes - 2, F32(FAR), F32(0))
        self.f_dn1 = jnp.where(lane >= 1, F32(-FAR), F32(0))
        self.b_dn1 = jnp.where(lane >= 1, F32(-NEAR), F32(0))
        self.b_dn2 = jnp.where(lane >= 2, F32(-FAR), F32(0))
        self.b_up1 = jnp.where(lane < lanes - 1, F32(FAR), F32(0))

    def fz(self, f):
        n = self.lanes
        return (self.f_up1 * pltpu.roll(f, n - 1, 1) - NEAR * f) + (
            self.f_up2 * pltpu.roll(f, n - 2, 1) + self.f_dn1 * pltpu.roll(f, 1, 1)
        )

    def bz(self, f):
        n = self.lanes
        return (self.b_dn1 * pltpu.roll(f, 1, 1) + NEAR * f) + (
            self.b_up1 * pltpu.roll(f, n - 1, 1) + self.b_dn2 * pltpu.roll(f, 2, 1)
        )


def fwd(at):
    return NEAR * (at(1) - at(0)) + FAR * (at(2) - at(-1))


def bwd(at):
    return NEAR * (at(0) - at(-1)) + FAR * (at(1) - at(-2))


def tile_reader(ref, field, start):
    seen = {}

    def read(layer, dy=0):
        if (layer, dy) not in seen:
            seen[layer, dy] = ref[field, layer, pl.ds(start + PAD + dy, ROWS), :]
        return seen[layer, dy]

    return read


def factors(active_cells, damp):
    return jnp.where(active_cells, damp, F32(1)), jnp.where(active_cells, DT * damp, F32(0))


def mask_rows(refs, moment, slab, start, blocks, block_rows):
    row = (moment * 3 + slab) * blocks + start // block_rows
    return jnp.broadcast_to(refs["mask"][pl.ds(row, 1), :], (ROWS, refs["mask"].shape[1])) > 0


def zero_pads(ref, rows):
    zeros = jnp.zeros((ref.shape[0], ref.shape[1], PAD, ref.shape[3]), F32)
    ref[:, :, :PAD, :] = zeros
    ref[:, :, PAD + rows:, :] = zeros


class Plan:
    def __init__(self, cx, rows, lanes, blocks, steps, cuts):
        self.cx, self.rows, self.lanes = cx, rows, lanes
        self.blocks, self.steps, self.cuts = blocks, steps, cuts
        self.block_rows = rows // blocks
        self.tiles = rows // ROWS

    def chunk(self, step, which):
        cut = self.cuts[step]
        return (0, cut) if which == 0 else (cut, self.tiles)

    def slots(self, step):
        n = self.cx
        if step < self.steps - 1:
            return [
                ((f, n + j), (f, REACH + j), (f, j), (f, n + REACH + j))
                for f in range(3) for j in range(REACH)
            ]
        top = [(0, n + 1), (0, n + 2), (1, n + 2), (2, n + 2), (2, n + 2)]
        bottom = [(0, 3), (1, 4), (1, 3), (2, 3), (2, 4)]
        below = [(0, 1), (0, 2), (1, 2), (2, 2), (2, 2)]
        above = [(0, n + 3), (1, n + 4), (1, n + 3), (2, n + 3), (2, n + 4)]
        return list(zip(top, bottom, below, above))

    def inner_forcing(self, refs, sh, so):
        z = Shifts(self.lanes)

        def tile(k, carry):
            start = pl.multiple_of(k * ROWS, ROWS)
            rows = pl.ds(start, ROWS)
            xy = tile_reader(sh, 1, start)
            xz = tile_reader(sh, 2, start)
            yy = tile_reader(so, 0, start)
            zz = tile_reader(so, 1, start)
            yz = tile_reader(so, 2, start)
            for i in range(self.cx):
                refs["inner"][0, i, rows, :] = bwd(lambda d: xy(i + 2, d)) + z.bz(xz(i + 2))
                refs["inner"][1, i, rows, :] = fwd(lambda d: yy(i, d)) + z.bz(yz(i))
                refs["inner"][2, i, rows, :] = bwd(lambda d: yz(i, d)) + z.fz(zz(i))
            return carry

        lax.fori_loop(0, self.tiles, tile, 0)

    def velocity(self, refs, moment, which, sh, so, previous):
        first, last = self.chunk(moment, which)
        z = Shifts(self.lanes)

        def tile(k, carry):
            start = pl.multiple_of(k * ROWS, ROWS)
            here = mask_rows(refs, moment, 1, start, self.blocks, self.block_rows)
            xx = tile_reader(sh, 0, start)
            xy = tile_reader(sh, 1, start)
            xz = tile_reader(sh, 2, start)
            yy = tile_reader(so, 0, start)
            zz = tile_reader(so, 1, start)
            yz = tile_reader(so, 2, start)
            rows = pl.ds(start, ROWS)
            for i in range(self.cx):
                keep, gain = factors(here, refs["damp"][i, pl.ds(start, ROWS), :])
                gain = gain * refs["buoy"][i, pl.ds(start, ROWS), :]
                gx = fwd(lambda d: xx(i + 1 + d))
                gy = bwd(lambda d: xy(i + 2 + d))
                gz = bwd(lambda d: xz(i + 2 + d))
                if "inner" in refs:
                    gx = gx + refs["inner"][0, i, rows, :]
                    gy = gy + refs["inner"][1, i, rows, :]
                    gz = gz + refs["inner"][2, i, rows, :]
                else:
                    gx = gx + bwd(lambda d: xy(i + 2, d)) + z.bz(xz(i + 2))
                    gy = gy + fwd(lambda d: yy(i, d)) + z.bz(yz(i))
                    gz = gz + bwd(lambda d: yz(i, d)) + z.fz(zz(i))
                for f, g in enumerate((gx, gy, gz)):
                    refs["vel_next"][f, REACH + i, pl.ds(start + PAD, ROWS), :] = (
                        keep * previous(f, i, start) + gain * g
                    )
            return carry

        lax.fori_loop(first, last, tile, 0)
        odd = odd_slab()
        rows = pl.ds(PAD + first * ROWS, (last - first) * ROWS)
        for slot, (top, bottom, _, _) in enumerate(self.slots(moment)):
            field, layer = pick(odd, top[0], bottom[0]), pick(odd, top[1], bottom[1])
            refs["send_far"][slot] = refs["vel_next"][field, layer, rows, :]
            field, layer = pick(odd, bottom[0], top[0]), pick(odd, bottom[1], top[1])
            refs["send_near"][slot] = refs["vel_next"][field, layer, rows, :]

    def arrivals(self, refs, moment, which):
        first, last = self.chunk(moment, which)
        odd = odd_slab()
        rows = pl.ds(PAD + first * ROWS, (last - first) * ROWS)
        for slot, (_, _, below, above) in enumerate(self.slots(moment)):
            field, layer = pick(odd, above[0], below[0]), pick(odd, above[1], below[1])
            refs["vel"][field, layer, rows, :] = refs["from_far"][slot]
            field, layer = pick(odd, below[0], above[0]), pick(odd, below[1], above[1])
            refs["vel"][field, layer, rows, :] = refs["from_near"][slot]

    def stress_tiles(self, moment, which):
        first, last = self.chunk(moment, which)
        if which == 1:
            return first - 1, last
        return first, last - 1 if moment == self.steps - 1 else last

    def stress(self, refs, moment, which, final, part=None):
        first, last = part or self.stress_tiles(moment, which)
        base = self.stress_tiles(moment, which)[0]
        n = self.cx
        z = Shifts(self.lanes)
        old_h, old_o = refs["sh"], refs["so"]

        def tile(k, carry):
            start = pl.multiple_of(k * ROWS, ROWS)
            masks = [mask_rows(refs, moment, slab, start, self.blocks, self.block_rows) for slab in range(3)]
            vx = tile_reader(refs["vel"], 0, start)
            vy = tile_reader(refs["vel"], 1, start)
            vz = tile_reader(refs["vel"], 2, start)
            rows = pl.ds(start, ROWS)
            padded = pl.ds(start + PAD, ROWS)

            def put_h(field, i, value):
                if final:
                    refs["done"][(0, 3, 4)[field], i, pl.ds(start - base * ROWS, ROWS), :] = value
                else:
                    refs["sh_next"][field, i + (1, 2, 2)[field], padded, :] = value

            def put_o(field, i, value):
                if final:
                    refs["done"][(1, 2, 5)[field], i, pl.ds(start - base * ROWS, ROWS), :] = value
                else:
                    refs["so_next"][field, i, padded, :] = value

            for i in range(0, n) if final else range(-2, n + 2):
                own = 0 <= i < n
                if own:
                    damp = refs["damp"][i, rows, :]
                else:
                    damp = refs["damp_edge"][i + 2 if i < 0 else i - n + 2, rows, :]
                keep, gain = factors(masks[0 if i < 0 else 1 if own else 2], damp)
                at = i + REACH
                mu = gain * refs["mu"][i + 2, rows, :]
                if i >= -1:
                    ex = bwd(lambda d: vx(at + d))
                    ey = bwd(lambda d: vy(at, d))
                    ez = z.bz(vz(at))
                    spread = gain * refs["lam"][i + 1, rows, :] * (ex + ey + ez)
                    mu2 = mu + mu
                    put_h(0, i, keep * old_h[0, i + 1, padded, :] + (spread + mu2 * ex))
                if own:
                    put_o(0, i, keep * old_o[0, i, padded, :] + (spread + mu2 * ey))
                    put_o(1, i, keep * old_o[1, i, padded, :] + (spread + mu2 * ez))
                    yz = z.fz(vy(at)) + fwd(lambda d: vz(at, d))
                    put_o(2, i, keep * old_o[2, i, padded, :] + mu * yz)
                if i <= n:
                    xy = fwd(lambda d: vx(at, d)) + fwd(lambda d: vy(at + d))
                    put_h(1, i, keep * old_h[1, i + 2, padded, :] + mu * xy)
                    xz = z.fz(vx(at)) + fwd(lambda d: vz(at + d))
                    put_h(2, i, keep * old_h[2, i + 2, padded, :] + mu * xz)
            return carry

        lax.fori_loop(first, last, tile, 0)

    def finish(self, refs, moment, which, done, sems):
        refs = dict(refs, done=done)
        first, last = self.stress_tiles(moment, which)
        copies = []

        def move(src, dst):
            copy = pltpu.make_async_copy(src, dst, sems.at[len(copies)])
            copy.start()
            copies.append(copy)

        for f in range(3):
            span = (last - first) * ROWS
            move(refs["vel"].at[f, pl.ds(REACH, self.cx), pl.ds(PAD + first * ROWS, span)],
                 refs["out"].at[0, f, :, pl.ds(first * ROWS, span)])
        for a, b in self.parts(first, last):
            self.stress(refs, moment, which, True, (a, b))
            span = (b - a) * ROWS
            for f in range(6):
                move(done.at[f, :, pl.ds((a - first) * ROWS, span)],
                     refs["out"].at[0, 3 + f, :, pl.ds(a * ROWS, span)])
        for copy in copies:
            copy.wait()

    @staticmethod
    def parts(first, last):
        middle = (first + last + 1) // 2
        return [(a, b) for a, b in ((first, middle), (middle, last)) if b > a]


STRESS_SLOTS = 5
MODEL_SLOTS = 6


def mover(sems):
    copies = []

    def move(src, dst):
        copy = pltpu.make_async_copy(src, dst, sems.at[len(copies)])
        copy.start()
        copies.append(copy)

    return move, copies


def pack(cx, refs, sems):
    odd = odd_slab()
    move, copies = mover(sems)
    for i, name in enumerate(("buoy", "q", "lam", "mu")):
        move(refs[name], refs["first" if i < 2 else "second"].at[pl.ds(i % 2 * cx, cx)])
    for slot, name in enumerate(("lam", "lam", "mu", "mu", "q", "q")):
        move(refs[name].at[pick(odd, cx - 2 + slot % 2, slot % 2)], refs["edge"].at[slot])
    top = [(3, cx - 1), (6, cx - 2), (6, cx - 1), (7, cx - 2), (7, cx - 1)]
    bottom = [(3, 0), (3, 1), (6, 0), (7, 0), (7, 0)]
    for name, flag in (("near", jnp.logical_not(odd)), ("far", odd)):
        for slot in range(STRESS_SLOTS):
            field = pick(flag, top[slot][0], bottom[slot][0])
            layer = pick(flag, top[slot][1], bottom[slot][1])
            move(refs["wave"].at[0, field, layer], refs[name].at[slot])
    for copy in copies:
        copy.wait()


def prepare(plan, refs):
    cx, rows = plan.cx, plan.rows
    zero_pads(refs["sh"], rows)
    zero_pads(refs["so"], rows)
    inner = pl.ds(PAD, rows)
    for field, (source, shift) in enumerate(((3, 1), (6, 2), (7, 2))):
        for i in range(cx):
            refs["sh"][field, i + shift, inner, :] = refs["wave"][0, source, i]
    for field, source in enumerate((4, 5, 8)):
        for i in range(cx):
            refs["so"][field, i, inner, :] = refs["wave"][0, source, i]
    for field in range(3):
        for i in range(cx):
            refs["old"][field, i] = refs["wave"][0, field, i]
    plan.inner_forcing(refs, refs["sh"], refs["so"])
    refs["ready"][...] = jnp.zeros(refs["ready"].shape, F32)


def after(array, *others):
    return lax.optimization_barrier((array,) + others)[0]


def spread(mine, shots):
    pairs = lambda k: [(i, i ^ k) for i in range(shots)]
    if shots == 4:
        beside = lax.ppermute(mine, "shot", pairs(1))
        across = lax.ppermute(mine, "shot", pairs(3))

        def finish(*others):
            handed = lax.ppermute(after(across, beside, *others), "shot", pairs(1))
            return {0: mine, 1: beside, 2: handed, 3: across}

        return (beside, across), finish
    turn = lambda k: [(i, (i + k) % shots) for i in range(shots)]
    swap = shots & (shots - 1) == 0
    got = {k: lax.ppermute(mine, "shot", pairs(k) if swap else turn(k)) for k in range(1, shots)}
    return tuple(got.values()), lambda *others: {0: mine, **got}


def origin_of(index, k, shots):
    if shots & (shots - 1) == 0:
        return index ^ k
    return lax.rem(index + shots - k, shots)


def panel_place(k, shots, panel_rows):
    start = origin_of(lax.axis_index("shot"), k, shots) * panel_rows
    return pl.ds(pl.multiple_of(start, panel_rows), panel_rows)


def per_device(cuts_of, shots, slabs, wave, lam, mu, buoy, q, active):
    cx, panel_rows, lanes = lam.shape
    rows = wave.shape[3]
    steps, _, blocks, lane_blocks = active.shape
    plan = Plan(cx, rows, lanes, blocks, steps, cuts_of(steps, rows // ROWS))
    padded = rows + 2 * PAD
    far = [(i, i + 1) for i in range(1, slabs - 1, 2)]
    near = [(i, i + 1) for i in range(0, slabs - 1, 2)]
    far = far + [(j, i) for i, j in far]
    near = near + [(j, i) for i, j in near]

    def exchange(to_far, to_near):
        return lax.ppermute(to_far, "aper", far), lax.ppermute(to_near, "aper", near)

    panel = (panel_rows, lanes)
    sent = call(
        functools.partial(pack, cx),
        dict(lam=lam, mu=mu, buoy=buoy, q=q, wave=wave),
        dict(first=(2 * cx,) + panel, second=(2 * cx,) + panel, edge=(MODEL_SLOTS,) + panel,
             far=(STRESS_SLOTS, rows, lanes), near=(STRESS_SLOTS, rows, lanes)),
        scratch=[pltpu.SemaphoreType.DMA((4 + MODEL_SLOTS + 2 * STRESS_SLOTS,))],
        anywhere=("lam", "mu", "buoy", "q", "wave"), us=0.02,
    )
    halo_far, halo_near = exchange(sent["far"], sent["near"])
    edge = lax.ppermute(sent["edge"], "aper", far)
    device = lax.axis_index("aper")
    around = lax.dynamic_slice_in_dim(jnp.pad(active, ((0, 0), (1, 1), (0, 0), (0, 0))), device, 3, 1)
    mask = jnp.repeat(around.astype(F32).reshape(steps * 3 * blocks, lane_blocks), lanes // lane_blocks, axis=1)

    sh_shape, so_shape = (3, cx + 3, padded, lanes), (3, cx, padded, lanes)
    vel_shape, slab_shape = (3, cx + 2 * REACH, padded, lanes), (cx, rows, lanes)
    state = call(functools.partial(prepare, plan), dict(wave=wave),
                 dict(sh=sh_shape, so=so_shape, old=(3,) + slab_shape, inner=(3,) + slab_shape, ready=(ROWS, lanes)), us=0.02)

    first_stage, finish = spread(sent["first"], shots)
    firsts = finish(halo_near, edge, mask, state["ready"])
    second = jnp.concatenate([sent["second"], after(edge, *first_stage)])
    _, finish_second = spread(second, shots)

    def sends(step, which):
        first, last = plan.chunk(step, which)
        shape = (len(plan.slots(step)), (last - first) * ROWS, lanes)
        return dict(send_far=shape, send_near=shape)

    def start_first(refs):
        odd = odd_slab()
        inner = pl.ds(PAD, rows)
        below = [(0, 0), (1, 0), (1, 1), (2, 0), (2, 1)]
        above = [(0, cx + 1), (0, cx + 2), (1, cx + 2), (2, cx + 2), (2, cx + 2)]
        for slot in range(STRESS_SLOTS):
            field = pick(odd, above[slot][0], below[slot][0])
            layer = pick(odd, above[slot][1], below[slot][1])
            refs["sh"][field, layer, inner, :] = refs["halo_far"][slot]
            field = pick(odd, below[slot][0], above[slot][0])
            layer = pick(odd, below[slot][1], above[slot][1])
            refs["sh"][field, layer, inner, :] = refs["halo_near"][slot]
        for k in firsts:
            place, got = panel_place(k, shots, panel_rows), refs["first%d" % k]
            for i in range(cx):
                refs["buoy"][i, place, :] = got[i]
                refs["damp"][i, place, :] = jnp.exp(-DT * got[cx + i])
        zero_pads(refs["vel_next"], rows)
        start_chunk(refs, 0)

    def start_chunk(refs, which):
        plan.velocity(refs, 0, which, refs["sh"], refs["so"],
                      lambda f, i, start: refs["old"][f, i, pl.ds(start, ROWS), :])

    ins = dict(halo_far=halo_far, halo_near=halo_near, mask=mask,
               **{name: state[name] for name in ("sh", "so", "old", "inner")})
    ins.update({"first%d" % k: a for k, a in firsts.items()})
    got = call(start_first, ins,
               dict(sh=sh_shape, buoy=slab_shape, damp=slab_shape, vel_next=vel_shape,
                    **sends(0, 0)),
               alias=("sh",), us=1.2)
    sh, so = got["sh"], state["so"]
    model = dict(mask=mask, buoy=got["buoy"], damp=got["damp"])
    arrived = [exchange(got["send_far"], got["send_near"])]
    got = call(lambda refs: start_chunk(refs, 1),
               dict(sh=sh, so=so, old=state["old"], inner=state["inner"], vel_next=got["vel_next"], **model),
               dict(vel_next=vel_shape, **sends(0, 1)), alias=("vel_next",), us=0.8)
    vel = got["vel_next"]
    arrived.append(exchange(got["send_far"], got["send_near"]))

    seconds = finish_second()

    def put_edge(refs, from_above, place, part):
        for j in range(2):
            refs["lam"][pick(from_above, cx + 1 + j, 0), place, :] = part(j)
            refs["mu"][pick(from_above, cx + 2 + j, j), place, :] = part(2 + j)
            refs["damp_edge"][pick(from_above, 2 + j, j), place, :] = part(4 + j)

    def assemble(refs):
        odd = odd_slab()
        for k in seconds:
            place, got = panel_place(k, shots, panel_rows), refs["second%d" % k]
            for i in range(cx):
                refs["lam"][i + 1, place, :] = got[i]
                refs["mu"][i + 2, place, :] = got[cx + i]
            put_edge(refs, odd, place, lambda slot: jnp.exp(-DT * got[2 * cx + slot])
                     if slot >= 4 else got[2 * cx + slot])
        for j in range(2):
            at = pick(odd, j, cx - 2 + j)
            refs["send_model"][j] = refs["lam"][at + 1]
            refs["send_model"][2 + j] = refs["mu"][at + 2]
            refs["send_model"][4 + j] = refs["damp"][at]

    edges = dict(lam=(cx + 3, rows, lanes), mu=(cx + 4, rows, lanes), damp_edge=(4, rows, lanes))
    got = call(assemble, dict(damp=model["damp"], **{"second%d" % k: a for k, a in seconds.items()}),
               dict(send_model=(MODEL_SLOTS, rows, lanes), **edges), us=0.02, waits=(arrived[1][1],))
    model_near = lax.ppermute(got["send_model"], "aper", near)
    model.update({name: got[name] for name in edges})
    vel = call(lambda refs: plan.arrivals(refs, 0, 0),
               dict(vel=vel, from_far=arrived[0][0], from_near=arrived[0][1]),
               dict(vel=vel_shape), alias=("vel",), us=20.0)["vel"]

    out_shape = wave.shape
    for step in range(steps):
        final = step == steps - 1

        def advance(refs, *scratch, which, step=step, final=final):
            if step == 0 and which == 0:
                put_edge(refs, jnp.logical_not(odd_slab()), slice(None), lambda slot: refs["model_near"][slot])
            else:
                plan.arrivals(refs, step, which)
            if final:
                plan.finish(refs, step, which, *scratch)
                return
            if which == 0:
                zero_pads(refs["sh_next"], rows)
                zero_pads(refs["so_next"], rows)
                zero_pads(refs["vel_next"], rows)
            plan.stress(refs, step, which, False)
            plan.velocity(
                refs, step + 1, which, refs["sh_next"], refs["so_next"],
                lambda f, i, start: refs["vel"][f, REACH + i, pl.ds(start + PAD, ROWS), :])

        nexts = dict(out=out_shape) if final else dict(
            sh_next=sh_shape, so_next=so_shape, vel_next=vel_shape)
        following = []
        carried = {}
        for which in range(2):
            ins = dict(vel=vel, sh=sh, so=so, from_far=arrived[which][0], from_near=arrived[which][1],
                       **model, **carried)
            outs = dict(vel=vel_shape, **nexts)
            if step == 0 and which == 0:
                ins.update(model_near=model_near)
                outs.update(edges)
            scratch = []
            if final:
                first, last = plan.stress_tiles(step, which)
                scratch = [pltpu.VMEM((6, cx, (last - first) * ROWS, lanes), F32),
                           pltpu.SemaphoreType.DMA((3 + 6 * len(plan.parts(first, last)),))]
            else:
                outs.update(sends(step + 1, which))
            got = call(functools.partial(advance, which=which), ins, outs, alias=("vel",) + tuple(carried) + (tuple(edges) if step + which == 0 else ()),
                       scratch=scratch, anywhere=("out",))
            vel = got["vel"]
            if step == 0 and which == 0:
                model.update({name: got[name] for name in edges})
            carried = {name: got[name] for name in nexts}
            if not final:
                following.append(exchange(got["send_far"], got["send_near"]))
        if final:
            return carried["out"]
        vel, sh, so, arrived = carried["vel_next"], carried["sh_next"], carried["so_next"], following


def cuts_of(steps, tiles):
    middle = tiles // 2 + steps // 2
    return [max(1, middle - step) for step in range(steps)]


def solution(mesh):
    body = functools.partial(per_device, cuts_of, mesh.shape["shot"], mesh.shape["aper"])
    return jax.shard_map(
        body,
        mesh=mesh,
        in_specs=(
            P("shot", None, "aper", None, None),
            P("aper", "shot", None),
            P("aper", "shot", None),
            P("aper", "shot", None),
            P("aper", "shot", None),
            P(),
        ),
        out_specs=P("shot", None, "aper", None, None),
        check_vma=False,
    )
```

```python
import functools

import jax
import jax.numpy as jnp
from jax import lax
from jax.experimental import pallas as pl
from jax.experimental.pallas import tpu as pltpu
from jax.sharding import PartitionSpec as P

NEAR = 1.125
FAR = -1.0 / 24.0
RATIO = FAR / NEAR
DT = 0.2
ROWS = 8
PAD = 8
REACH = 3
VMEM = pl.BlockSpec(memory_space=pltpu.VMEM)
ANY = pl.BlockSpec(memory_space=pl.ANY)
F32 = jnp.float32


def call(body, ins, outs, alias=(), scratch=(), anywhere=(), us=5.0, waits=()):
    ins = dict(ins, **{"wait%d" % i: a for i, a in enumerate(waits)})
    in_names, out_names = list(ins), list(outs)

    def kernel(*refs):
        names = {}
        for name, ref in zip(in_names, refs):
            if name not in alias:
                names[name] = ref
        for name, ref in zip(out_names, refs[len(in_names):]):
            names[name] = ref
        body(names, *refs[len(in_names) + len(out_names):])

    ins = {name: pltpu.with_memory_space_constraint(a, pltpu.HBM) if name in anywhere
           else pltpu.with_memory_space_constraint(a, pltpu.VMEM) if name in alias
           else a for name, a in ins.items()}
    results = pl.pallas_call(
        kernel,
        out_shape=[pltpu.HBM(shape, F32) if name in anywhere else pltpu.VMEM(shape, F32)
                   for name, shape in outs.items()],
        in_specs=[ANY if name in anywhere or name[:4] == "wait" else VMEM for name in in_names],
        out_specs=[ANY if name in anywhere else VMEM for name in out_names],
        scratch_shapes=list(scratch),
        input_output_aliases={in_names.index(n): out_names.index(n) for n in alias},
        compiler_params=pltpu.CompilerParams(vmem_limit_bytes=24 * 2**20),
        cost_estimate=pl.CostEstimate(flops=int(us * 1e9), bytes_accessed=int(us * 3.6e6), transcendentals=0),
    )(*ins.values())
    return dict(zip(out_names, results))


def odd_slab():
    return lax.rem(lax.axis_index("aper"), 2) == 1


def pick(flag, yes, no):
    return jnp.where(flag, jnp.int32(yes), jnp.int32(no))


class Shifts:
    def __init__(self, lanes):
        lane = lax.broadcasted_iota(jnp.int32, (ROWS, lanes), 1)
        self.lanes = lanes
        self.f_up1 = jnp.where(lane < lanes - 1, F32(1), F32(0))
        self.f_up2 = jnp.where(lane < lanes - 2, F32(RATIO), F32(0))
        self.f_dn1 = jnp.where(lane >= 1, F32(RATIO), F32(0))
        self.b_dn1 = jnp.where(lane >= 1, F32(1), F32(0))
        self.b_dn2 = jnp.where(lane >= 2, F32(RATIO), F32(0))
        self.b_up1 = jnp.where(lane < lanes - 1, F32(RATIO), F32(0))

    def fz(self, f):
        n = self.lanes
        return (self.f_up1 * pltpu.roll(f, n - 1, 1) - f) + (
            self.f_up2 * pltpu.roll(f, n - 2, 1) - self.f_dn1 * pltpu.roll(f, 1, 1)
        )

    def bz(self, f):
        n = self.lanes
        return (f - self.b_dn1 * pltpu.roll(f, 1, 1)) + (
            self.b_up1 * pltpu.roll(f, n - 1, 1) - self.b_dn2 * pltpu.roll(f, 2, 1)
        )


def fwd(at):
    return (at(1) - at(0)) + RATIO * (at(2) - at(-1))


def bwd(at):
    return (at(0) - at(-1)) + RATIO * (at(1) - at(-2))


def tile_reader(ref, field, start):
    seen = {}

    def read(layer, dy=0):
        if (layer, dy) not in seen:
            seen[layer, dy] = ref[field, layer, pl.ds(start + PAD + dy, ROWS), :]
        return seen[layer, dy]

    return read


def factors(active_cells, damp):
    return jnp.where(active_cells, damp, F32(1)), jnp.where(active_cells, (DT * NEAR) * damp, F32(0))


def zero_pads(ref, rows):
    zeros = jnp.zeros((ref.shape[0], ref.shape[1], PAD, ref.shape[3]), F32)
    ref[:, :, :PAD, :] = zeros
    ref[:, :, PAD + rows:, :] = zeros


class Plan:
    def __init__(self, cx, rows, lanes, blocks, steps, slabs, cuts):
        self.slabs = slabs
        self.cx, self.rows, self.lanes = cx, rows, lanes
        self.blocks, self.steps, self.cuts = blocks, steps, cuts
        self.block_rows = rows // blocks
        self.tiles = rows // ROWS

    def active(self, refs, moment, side, start):
        slab = jnp.clip(lax.axis_index("aper") + side - 1, 0, self.slabs - 1)
        row = (moment * self.slabs + slab) * self.blocks + start // self.block_rows
        return jnp.broadcast_to(refs["mask"][pl.ds(row, 1), :], (ROWS, self.lanes)) > 0

    def chunk(self, step, which):
        cut = self.cuts[step]
        return (0, cut) if which == 0 else (cut, self.tiles)

    def slots(self, step):
        n = self.cx
        if step < self.steps - 1:
            return [
                ((f, n + j), (f, REACH + j), (f, j), (f, n + REACH + j))
                for f in range(3) for j in range(REACH)
            ]
        top = [(0, n + 1), (0, n + 2), (1, n + 2), (2, n + 2), (2, n + 2)]
        bottom = [(0, 3), (1, 4), (1, 3), (2, 3), (2, 4)]
        below = [(0, 1), (0, 2), (1, 2), (2, 2), (2, 2)]
        above = [(0, n + 3), (1, n + 4), (1, n + 3), (2, n + 3), (2, n + 4)]
        return list(zip(top, bottom, below, above))

    def inner_forcing(self, refs, sh, so):
        z = Shifts(self.lanes)

        def tile(k, carry):
            start = pl.multiple_of(k * ROWS, ROWS)
            rows = pl.ds(start, ROWS)
            xy = tile_reader(sh, 1, start)
            xz = tile_reader(sh, 2, start)
            yy = tile_reader(so, 0, start)
            zz = tile_reader(so, 1, start)
            yz = tile_reader(so, 2, start)
            for i in range(self.cx):
                refs["inner"][0, i, rows, :] = bwd(lambda d: xy(i + 2, d)) + z.bz(xz(i + 2))
                refs["inner"][1, i, rows, :] = fwd(lambda d: yy(i, d)) + z.bz(yz(i))
                refs["inner"][2, i, rows, :] = bwd(lambda d: yz(i, d)) + z.fz(zz(i))
            return carry

        lax.fori_loop(0, self.tiles, tile, 0)

    def velocity(self, refs, moment, which, sh, so, previous):
        first, last = self.chunk(moment, which)
        z = Shifts(self.lanes)

        def tile(k, carry):
            start = pl.multiple_of(k * ROWS, ROWS)
            here = self.active(refs, moment, 1, start)
            xx = tile_reader(sh, 0, start)
            xy = tile_reader(sh, 1, start)
            xz = tile_reader(sh, 2, start)
            yy = tile_reader(so, 0, start)
            zz = tile_reader(so, 1, start)
            yz = tile_reader(so, 2, start)
            rows = pl.ds(start, ROWS)
            for i in range(self.cx):
                keep, gain = factors(here, refs["damp"][i, pl.ds(start, ROWS), :])
                gain = gain * refs["buoy"][i, pl.ds(start, ROWS), :]
                gx = fwd(lambda d: xx(i + 1 + d))
                gy = bwd(lambda d: xy(i + 2 + d))
                gz = bwd(lambda d: xz(i + 2 + d))
                if "inner" in refs:
                    gx = gx + refs["inner"][0, i, rows, :]
                    gy = gy + refs["inner"][1, i, rows, :]
                    gz = gz + refs["inner"][2, i, rows, :]
                else:
                    gx = gx + bwd(lambda d: xy(i + 2, d)) + z.bz(xz(i + 2))
                    gy = gy + fwd(lambda d: yy(i, d)) + z.bz(yz(i))
                    gz = gz + bwd(lambda d: yz(i, d)) + z.fz(zz(i))
                for f, g in enumerate((gx, gy, gz)):
                    refs["vel_next"][f, REACH + i, pl.ds(start + PAD, ROWS), :] = (
                        keep * previous(f, i, start) + gain * g
                    )
            return carry

        lax.fori_loop(first, last, tile, 0, unroll=True)
        odd = odd_slab()
        rows = pl.ds(PAD + first * ROWS, (last - first) * ROWS)
        for slot, (top, bottom, _, _) in enumerate(self.slots(moment)):
            field, layer = pick(odd, top[0], bottom[0]), pick(odd, top[1], bottom[1])
            refs["send_far"][slot] = refs["vel_next"][field, layer, rows, :]
            field, layer = pick(odd, bottom[0], top[0]), pick(odd, bottom[1], top[1])
            refs["send_near"][slot] = refs["vel_next"][field, layer, rows, :]

    def arrivals(self, refs, moment, which):
        first, last = self.chunk(moment, which)
        odd = odd_slab()
        rows = pl.ds(PAD + first * ROWS, (last - first) * ROWS)
        for slot, (_, _, below, above) in enumerate(self.slots(moment)):
            field, layer = pick(odd, above[0], below[0]), pick(odd, above[1], below[1])
            refs["vel"][field, layer, rows, :] = refs["from_far"][slot]
            field, layer = pick(odd, below[0], above[0]), pick(odd, below[1], above[1])
            refs["vel"][field, layer, rows, :] = refs["from_near"][slot]

    def stress_tiles(self, moment, which):
        first, last = self.chunk(moment, which)
        if which == 1:
            return first - 1, last
        return first, last - 1 if moment == self.steps - 1 else last

    def stress(self, refs, moment, which, final, part=None):
        first, last = part or self.stress_tiles(moment, which)
        base = self.stress_tiles(moment, which)[0]
        n = self.cx
        z = Shifts(self.lanes)
        old_h, old_o = refs["sh"], refs["so"]

        def tile(k, carry):
            start = pl.multiple_of(k * ROWS, ROWS)
            masks = [self.active(refs, moment, side, start) for side in range(3)]
            vx = tile_reader(refs["vel"], 0, start)
            vy = tile_reader(refs["vel"], 1, start)
            vz = tile_reader(refs["vel"], 2, start)
            rows = pl.ds(start, ROWS)
            padded = pl.ds(start + PAD, ROWS)

            def put_h(field, i, value):
                if final:
                    refs["done"][(0, 3, 4)[field], i, pl.ds(start - base * ROWS, ROWS), :] = value
                else:
                    refs["sh_next"][field, i + (1, 2, 2)[field], padded, :] = value

            def put_o(field, i, value):
                if final:
                    refs["done"][(1, 2, 5)[field], i, pl.ds(start - base * ROWS, ROWS), :] = value
                else:
                    refs["so_next"][field, i, padded, :] = value

            for i in range(0, n) if final else range(-2, n + 2):
                own = 0 <= i < n
                if own:
                    damp = refs["damp"][i, rows, :]
                else:
                    damp = refs["damp_edge"][i + 2 if i < 0 else i - n + 2, rows, :]
                keep, gain = factors(masks[0 if i < 0 else 1 if own else 2], damp)
                at = i + REACH
                mu = gain * refs["mu"][i + 2, rows, :]
                if i >= -1:
                    ex = bwd(lambda d: vx(at + d))
                    ey = bwd(lambda d: vy(at, d))
                    ez = z.bz(vz(at))
                    spread = gain * refs["lam"][i + 1, rows, :] * (ex + ey + ez)
                    mu2 = mu + mu
                    put_h(0, i, keep * old_h[0, i + 1, padded, :] + (spread + mu2 * ex))
                if own:
                    put_o(0, i, keep * old_o[0, i, padded, :] + (spread + mu2 * ey))
                    put_o(1, i, keep * old_o[1, i, padded, :] + (spread + mu2 * ez))
                    yz = z.fz(vy(at)) + fwd(lambda d: vz(at, d))
                    put_o(2, i, keep * old_o[2, i, padded, :] + mu * yz)
                if i <= n:
                    xy = fwd(lambda d: vx(at, d)) + fwd(lambda d: vy(at + d))
                    put_h(1, i, keep * old_h[1, i + 2, padded, :] + mu * xy)
                    xz = z.fz(vx(at)) + fwd(lambda d: vz(at + d))
                    put_h(2, i, keep * old_h[2, i + 2, padded, :] + mu * xz)
            return carry

        lax.fori_loop(first, last, tile, 0, unroll=True)

    def finish(self, refs, moment, which, done, sems):
        refs = dict(refs, done=done)
        first, last = self.stress_tiles(moment, which)
        copies = []

        def move(src, dst):
            copy = pltpu.make_async_copy(src, dst, sems.at[len(copies)])
            copy.start()
            copies.append(copy)

        for f in range(3):
            span = (last - first) * ROWS
            move(refs["vel"].at[f, pl.ds(REACH, self.cx), pl.ds(PAD + first * ROWS, span)],
                 refs["out"].at[0, f, :, pl.ds(first * ROWS, span)])
        for a, b in self.parts(first, last):
            self.stress(refs, moment, which, True, (a, b))
            span = (b - a) * ROWS
            for f in range(6):
                move(done.at[f, :, pl.ds((a - first) * ROWS, span)],
                     refs["out"].at[0, 3 + f, :, pl.ds(a * ROWS, span)])
        for copy in copies:
            copy.wait()

    @staticmethod
    def parts(first, last):
        middle = (first + last + 1) // 2
        return [(a, b) for a, b in ((first, middle), (middle, last)) if b > a]


STRESS_SLOTS = 5
MODEL_SLOTS = 6


def mover(sems):
    copies = []

    def move(src, dst):
        copy = pltpu.make_async_copy(src, dst, sems.at[len(copies)])
        copy.start()
        copies.append(copy)

    return move, copies


def pack_model(cx, refs, sems):
    odd = odd_slab()
    move, copies = mover(sems)
    for i, name in enumerate(("buoy", "q")):
        move(refs[name], refs["first"].at[pl.ds(i * cx, cx)])
    for i, name in enumerate(("lam", "mu", "q")):
        move(refs[name].at[pl.ds(pick(odd, cx - 2, 0), 2)], refs["edge"].at[pl.ds(2 * i, 2)])
    for i, name in enumerate(("lam", "mu")):
        move(refs[name], refs["second"].at[pl.ds(i * cx, cx)])
    for copy in copies:
        copy.wait()


def pack_stress(cx, refs, sems):
    odd = odd_slab()
    move, copies = mover(sems)
    top = [(3, cx - 1), (6, cx - 2), (6, cx - 1), (7, cx - 2), (7, cx - 1)]
    bottom = [(3, 0), (3, 1), (6, 0), (7, 0), (7, 0)]
    for name, flag in (("near", jnp.logical_not(odd)), ("far", odd)):
        for slot in range(STRESS_SLOTS):
            field = pick(flag, top[slot][0], bottom[slot][0])
            layer = pick(flag, top[slot][1], bottom[slot][1])
            move(refs["wave"].at[0, field, layer], refs[name].at[slot])
    for copy in copies:
        copy.wait()


def prepare(plan, refs):
    cx, rows = plan.cx, plan.rows
    zero_pads(refs["sh"], rows)
    zero_pads(refs["so"], rows)
    inner = pl.ds(PAD, rows)
    for field, (source, shift) in enumerate(((3, 1), (6, 2), (7, 2))):
        for i in range(cx):
            refs["sh"][field, i + shift, inner, :] = refs["wave"][0, source, i]
    for field, source in enumerate((4, 5, 8)):
        for i in range(cx):
            refs["so"][field, i, inner, :] = refs["wave"][0, source, i]
    for field in range(3):
        for i in range(cx):
            refs["old"][field, i] = refs["wave"][0, field, i]
    plan.inner_forcing(refs, refs["sh"], refs["so"])
    lane_blocks = refs["active"].shape[1]
    block = lax.broadcasted_iota(jnp.int32, (lane_blocks, plan.lanes), 1) // (plan.lanes // lane_blocks)
    own = block == lax.broadcasted_iota(jnp.int32, (lane_blocks, plan.lanes), 0)
    refs["mask"][...] = jnp.dot(refs["active"][...].astype(F32), own.astype(F32),
                                preferred_element_type=F32)


def hold(array, *others):
    return call(lambda refs: None, dict(array=array), dict(array=array.shape), alias=("array",),
                us=0.02, waits=others)["array"]


def spread(mine, shots):
    pairs = lambda k: [(i, i ^ k) for i in range(shots)]
    if shots == 4:
        beside = lax.ppermute(mine, "shot", pairs(1))
        across = lax.ppermute(mine, "shot", pairs(3))

        def finish(*others):
            handed = lax.ppermute(hold(across, beside, *others), "shot", pairs(1))
            return {0: mine, 1: beside, 2: handed, 3: across}

        return (beside, across), finish
    turn = lambda k: [(i, (i + k) % shots) for i in range(shots)]
    swap = shots & (shots - 1) == 0
    got = {k: lax.ppermute(mine, "shot", pairs(k) if swap else turn(k)) for k in range(1, shots)}
    return tuple(got.values()), lambda *others: {0: mine, **got}


def origin_of(index, k, shots):
    if shots & (shots - 1) == 0:
        return index ^ k
    return lax.rem(index + shots - k, shots)


def panel_place(k, shots, panel_rows):
    start = origin_of(lax.axis_index("shot"), k, shots) * panel_rows
    return pl.ds(pl.multiple_of(start, panel_rows), panel_rows)


def per_device(cuts_of, shots, slabs, wave, lam, mu, buoy, q, active):
    cx, panel_rows, lanes = lam.shape
    rows = wave.shape[3]
    steps, _, blocks, lane_blocks = active.shape
    plan = Plan(cx, rows, lanes, blocks, steps, slabs, cuts_of(steps, rows // ROWS))
    padded = rows + 2 * PAD
    far = [(i, i + 1) for i in range(1, slabs - 1, 2)]
    near = [(i, i + 1) for i in range(0, slabs - 1, 2)]
    far = far + [(j, i) for i, j in far]
    near = near + [(j, i) for i, j in near]

    def exchange(to_far, to_near):
        return lax.ppermute(to_far, "aper", far), lax.ppermute(to_near, "aper", near)

    panel = (panel_rows, lanes)
    sent = call(
        functools.partial(pack_model, cx), dict(lam=lam, mu=mu, buoy=buoy, q=q),
        dict(first=(2 * cx,) + panel, second=(2 * cx,) + panel, edge=(MODEL_SLOTS,) + panel),
        scratch=[pltpu.SemaphoreType.DMA((7,))], anywhere=("lam", "mu", "buoy", "q"), us=0.02,
    )
    sent.update(call(
        functools.partial(pack_stress, cx), dict(wave=wave),
        dict(far=(STRESS_SLOTS, rows, lanes), near=(STRESS_SLOTS, rows, lanes)),
        scratch=[pltpu.SemaphoreType.DMA((2 * STRESS_SLOTS,))], anywhere=("wave",), us=5.0, waits=(sent["edge"],),
    ))
    halo_far, halo_near = exchange(sent["far"], sent["near"])
    edge = lax.ppermute(sent["edge"], "aper", far)
    sh_shape, so_shape = (3, cx + 3, padded, lanes), (3, cx, padded, lanes)
    vel_shape, slab_shape = (3, cx + 2 * REACH, padded, lanes), (cx, rows, lanes)
    state = call(functools.partial(prepare, plan), dict(wave=wave, active=active.reshape(-1, lane_blocks)),
                 dict(sh=sh_shape, so=so_shape, old=(3,) + slab_shape, inner=(3,) + slab_shape, mask=(steps * slabs * blocks, lanes)), us=5.0)

    first_stage, finish = spread(sent["first"], shots)
    mask = state["mask"]
    firsts = finish(edge)

    def join(refs):
        refs["all"][:2 * cx] = refs["second"][...]
        refs["all"][2 * cx:] = refs["edge"][...]

    second = call(join, dict(second=sent["second"], edge=edge),
                  dict(all=(2 * cx + MODEL_SLOTS,) + panel), us=0.02, waits=first_stage + (mask,))["all"]
    _, finish_second = spread(second, shots)

    def sends(step, which):
        first, last = plan.chunk(step, which)
        shape = (len(plan.slots(step)), (last - first) * ROWS, lanes)
        return dict(send_far=shape, send_near=shape)

    def start_first(refs):
        odd = odd_slab()
        inner = pl.ds(PAD, rows)
        below = [(0, 0), (1, 0), (1, 1), (2, 0), (2, 1)]
        above = [(0, cx + 1), (0, cx + 2), (1, cx + 2), (2, cx + 2), (2, cx + 2)]
        for slot in range(STRESS_SLOTS):
            field = pick(odd, above[slot][0], below[slot][0])
            layer = pick(odd, above[slot][1], below[slot][1])
            refs["sh"][field, layer, inner, :] = refs["halo_far"][slot]
            field = pick(odd, below[slot][0], above[slot][0])
            layer = pick(odd, below[slot][1], above[slot][1])
            refs["sh"][field, layer, inner, :] = refs["halo_near"][slot]
        for k in firsts:
            place, got = panel_place(k, shots, panel_rows), refs["first%d" % k]
            for i in range(cx):
                refs["buoy"][i, place, :] = got[i]
                refs["damp"][i, place, :] = jnp.exp(-DT * got[cx + i])
        zero_pads(refs["vel_next"], rows)
        start_chunk(refs, 0)

    def start_chunk(refs, which):
        plan.velocity(refs, 0, which, refs["sh"], refs["so"],
                      lambda f, i, start: refs["old"][f, i, pl.ds(start, ROWS), :])

    ins = dict(halo_far=halo_far, halo_near=halo_near, **state)
    ins.update({"first%d" % k: a for k, a in firsts.items()})
    got = call(start_first, ins,
               dict(sh=sh_shape, buoy=slab_shape, damp=slab_shape, vel_next=vel_shape,
                    **sends(0, 0)),
               alias=("sh",), us=1.2)
    sh, so = got["sh"], state["so"]
    model = dict(mask=mask, buoy=got["buoy"], damp=got["damp"])
    arrived = [exchange(got["send_far"], got["send_near"])]
    got = call(lambda refs: start_chunk(refs, 1),
               dict(sh=sh, so=so, old=state["old"], inner=state["inner"], vel_next=got["vel_next"], **model),
               dict(vel_next=vel_shape, **sends(0, 1)), alias=("vel_next",), us=0.8)
    vel = got["vel_next"]
    arrived.append(exchange(got["send_far"], got["send_near"]))

    seconds = finish_second()

    def put_edge(refs, from_above, place, part):
        for j in range(2):
            refs["lam"][pick(from_above, cx + 1 + j, 0), place, :] = part(j)
            refs["mu"][pick(from_above, cx + 2 + j, j), place, :] = part(2 + j)
            refs["damp_edge"][pick(from_above, 2 + j, j), place, :] = part(4 + j)

    def assemble(refs):
        odd = odd_slab()
        for k in seconds:
            place, got = panel_place(k, shots, panel_rows), refs["second%d" % k]
            for i in range(cx):
                refs["lam"][i + 1, place, :] = got[i]
                refs["mu"][i + 2, place, :] = got[cx + i]
            put_edge(refs, odd, place, lambda slot: jnp.exp(-DT * got[2 * cx + slot])
                     if slot >= 4 else got[2 * cx + slot])
        for j in range(2):
            at = pick(odd, j, cx - 2 + j)
            refs["send_model"][j] = refs["lam"][at + 1]
            refs["send_model"][2 + j] = refs["mu"][at + 2]
            refs["send_model"][4 + j] = refs["damp"][at]

    edges = dict(lam=(cx + 3, rows, lanes), mu=(cx + 4, rows, lanes), damp_edge=(4, rows, lanes))
    got = call(assemble, dict(damp=model["damp"], **{"second%d" % k: a for k, a in seconds.items()}),
               dict(send_model=(MODEL_SLOTS, rows, lanes), **edges), us=0.02, waits=(arrived[1][1],))
    model_near = lax.ppermute(got["send_model"], "aper", near)
    model.update({name: got[name] for name in edges})
    vel = call(lambda refs: plan.arrivals(refs, 0, 0),
               dict(vel=vel, from_far=arrived[0][0], from_near=arrived[0][1]),
               dict(vel=vel_shape), alias=("vel",), us=20.0)["vel"]

    out_shape = wave.shape
    for step in range(steps):
        final = step == steps - 1

        def advance(refs, *scratch, which, step=step, final=final):
            if step == 0 and which == 0:
                put_edge(refs, jnp.logical_not(odd_slab()), slice(None), lambda slot: refs["model_near"][slot])
            else:
                plan.arrivals(refs, step, which)
            if final:
                plan.finish(refs, step, which, *scratch)
                return
            if which == 0:
                zero_pads(refs["sh_next"], rows)
                zero_pads(refs["so_next"], rows)
                zero_pads(refs["vel_next"], rows)
            plan.stress(refs, step, which, False)
            plan.velocity(
                refs, step + 1, which, refs["sh_next"], refs["so_next"],
                lambda f, i, start: refs["vel"][f, REACH + i, pl.ds(start + PAD, ROWS), :])

        nexts = dict(out=out_shape) if final else dict(
            sh_next=sh_shape, so_next=so_shape, vel_next=vel_shape)
        following = []
        carried = {}
        for which in range(2):
            ins = dict(vel=vel, sh=sh, so=so, from_far=arrived[which][0], from_near=arrived[which][1],
                       **model, **carried)
            outs = dict(vel=vel_shape, **nexts)
            if step == 0 and which == 0:
                ins.update(model_near=model_near)
                outs.update(edges)
            scratch = []
            if final:
                first, last = plan.stress_tiles(step, which)
                scratch = [pltpu.VMEM((6, cx, (last - first) * ROWS, lanes), F32),
                           pltpu.SemaphoreType.DMA((3 + 6 * len(plan.parts(first, last)),))]
            else:
                outs.update(sends(step + 1, which))
            got = call(functools.partial(advance, which=which), ins, outs, alias=("vel",) + tuple(carried) + (tuple(edges) if step + which == 0 else ()),
                       scratch=scratch, anywhere=("out",))
            vel = got["vel"]
            if step == 0 and which == 0:
                model.update({name: got[name] for name in edges})
            carried = {name: got[name] for name in nexts}
            if not final:
                following.append(exchange(got["send_far"], got["send_near"]))
        if final:
            return carried["out"]
        vel, sh, so, arrived = carried["vel_next"], carried["sh_next"], carried["so_next"], following


def cuts_of(steps, tiles):
    middle = tiles // 2 + 1
    return [max(1, middle - step) for step in range(steps)]


def solution(mesh):
    body = functools.partial(per_device, cuts_of, mesh.shape["shot"], mesh.shape["aper"])
    return jax.shard_map(
        body,
        mesh=mesh,
        in_specs=(
            P("shot", None, "aper", None, None),
            P("aper", "shot", None),
            P("aper", "shot", None),
            P("aper", "shot", None),
            P("aper", "shot", None),
            P(),
        ),
        out_specs=P("shot", None, "aper", None, None),
        check_vma=False,
    )
```

```python
import functools

import jax
import jax.numpy as jnp
from jax import lax
from jax.experimental import pallas as pl
from jax.experimental.pallas import tpu as pltpu
from jax.sharding import PartitionSpec as P

NEAR = 1.125
FAR = -1.0 / 24.0
RATIO = FAR / NEAR
DT = 0.2
ROWS = 8
PAD = 8
REACH = 3
VMEM = pl.BlockSpec(memory_space=pltpu.VMEM)
ANY = pl.BlockSpec(memory_space=pl.ANY)
F32 = jnp.float32


def call(body, ins, outs, alias=(), scratch=(), anywhere=(), us=5.0, waits=()):
    ins = dict(ins, **{"wait%d" % i: a for i, a in enumerate(waits)})
    in_names, out_names = list(ins), list(outs)

    def kernel(*refs):
        names = {}
        for name, ref in zip(in_names, refs):
            if name not in alias:
                names[name] = ref
        for name, ref in zip(out_names, refs[len(in_names):]):
            names[name] = ref
        body(names, *refs[len(in_names) + len(out_names):])

    ins = {name: pltpu.with_memory_space_constraint(a, pltpu.HBM) if name in anywhere
           else pltpu.with_memory_space_constraint(a, pltpu.VMEM) if name in alias
           else a for name, a in ins.items()}
    results = pl.pallas_call(
        kernel,
        out_shape=[pltpu.HBM(shape, F32) if name in anywhere else pltpu.VMEM(shape, F32)
                   for name, shape in outs.items()],
        in_specs=[ANY if name in anywhere or name[:4] == "wait" else VMEM for name in in_names],
        out_specs=[ANY if name in anywhere else VMEM for name in out_names],
        scratch_shapes=list(scratch),
        input_output_aliases={in_names.index(n): out_names.index(n) for n in alias},
        compiler_params=pltpu.CompilerParams(vmem_limit_bytes=24 * 2**20),
        cost_estimate=pl.CostEstimate(flops=int(us * 1e9), bytes_accessed=int(us * 3.6e6), transcendentals=0),
    )(*ins.values())
    return dict(zip(out_names, results))


def odd_slab():
    return lax.rem(lax.axis_index("aper"), 2) == 1


def pick(flag, yes, no):
    return jnp.where(flag, jnp.int32(yes), jnp.int32(no))


class Shifts:
    def __init__(self, lanes):
        lane = lax.broadcasted_iota(jnp.int32, (ROWS, lanes), 1)
        self.lanes = lanes
        self.f_up1 = jnp.where(lane < lanes - 1, F32(1), F32(0))
        self.f_up2 = jnp.where(lane < lanes - 2, F32(RATIO), F32(0))
        self.f_dn1 = jnp.where(lane >= 1, F32(RATIO), F32(0))
        self.b_dn1 = jnp.where(lane >= 1, F32(1), F32(0))
        self.b_dn2 = jnp.where(lane >= 2, F32(RATIO), F32(0))
        self.b_up1 = jnp.where(lane < lanes - 1, F32(RATIO), F32(0))

    def fz(self, f):
        n = self.lanes
        return (self.f_up1 * pltpu.roll(f, n - 1, 1) - f) + (
            self.f_up2 * pltpu.roll(f, n - 2, 1) - self.f_dn1 * pltpu.roll(f, 1, 1)
        )

    def bz(self, f):
        n = self.lanes
        return (f - self.b_dn1 * pltpu.roll(f, 1, 1)) + (
            self.b_up1 * pltpu.roll(f, n - 1, 1) - self.b_dn2 * pltpu.roll(f, 2, 1)
        )


def fwd(at):
    return (at(1) - at(0)) + RATIO * (at(2) - at(-1))


def bwd(at):
    return (at(0) - at(-1)) + RATIO * (at(1) - at(-2))


def tile_reader(ref, field, start):
    seen = {}

    def read(layer, dy=0):
        if (layer, dy) not in seen:
            seen[layer, dy] = ref[field, layer, pl.ds(start + PAD + dy, ROWS), :]
        return seen[layer, dy]

    return read


def factors(active_cells, damp):
    return jnp.where(active_cells, damp, F32(1)), jnp.where(active_cells, (DT * NEAR) * damp, F32(0))


def zero_pads(ref, rows):
    zeros = jnp.zeros((ref.shape[0], ref.shape[1], PAD, ref.shape[3]), F32)
    ref[:, :, :PAD, :] = zeros
    ref[:, :, PAD + rows:, :] = zeros


class Plan:
    def __init__(self, cx, rows, lanes, blocks, steps, slabs, cuts):
        self.slabs = slabs
        self.cx, self.rows, self.lanes = cx, rows, lanes
        self.blocks, self.steps, self.cuts = blocks, steps, cuts
        self.block_rows = rows // blocks
        self.tiles = rows // ROWS

    def active(self, refs, moment, side, start):
        slab = jnp.clip(lax.axis_index("aper") + side - 1, 0, self.slabs - 1)
        row = (moment * self.slabs + slab) * self.blocks + start // self.block_rows
        return jnp.broadcast_to(refs["mask"][pl.ds(row, 1), :], (ROWS, self.lanes)) > 0

    def chunk(self, step, which):
        cut = self.cuts[step]
        return (0, cut) if which == 0 else (cut, self.tiles)

    def slots(self, step):
        n = self.cx
        if step < self.steps - 1:
            return [
                ((f, n + j), (f, REACH + j), (f, j), (f, n + REACH + j))
                for f in range(3) for j in range(REACH)
            ]
        top = [(0, n + 1), (0, n + 2), (1, n + 2), (2, n + 2), (2, n + 2)]
        bottom = [(0, 3), (1, 4), (1, 3), (2, 3), (2, 4)]
        below = [(0, 1), (0, 2), (1, 2), (2, 2), (2, 2)]
        above = [(0, n + 3), (1, n + 4), (1, n + 3), (2, n + 3), (2, n + 4)]
        return list(zip(top, bottom, below, above))

    def inner_forcing(self, refs, sh, so):
        z = Shifts(self.lanes)

        def tile(k, carry):
            start = pl.multiple_of(k * ROWS, ROWS)
            rows = pl.ds(start, ROWS)
            xy = tile_reader(sh, 1, start)
            xz = tile_reader(sh, 2, start)
            yy = tile_reader(so, 0, start)
            zz = tile_reader(so, 1, start)
            yz = tile_reader(so, 2, start)
            for i in range(self.cx):
                refs["inner"][0, i, rows, :] = bwd(lambda d: xy(i + 2, d)) + z.bz(xz(i + 2))
                refs["inner"][1, i, rows, :] = fwd(lambda d: yy(i, d)) + z.bz(yz(i))
                refs["inner"][2, i, rows, :] = bwd(lambda d: yz(i, d)) + z.fz(zz(i))
            return carry

        lax.fori_loop(0, self.tiles, tile, 0)

    def velocity(self, refs, moment, which, sh, so, previous):
        first, last = self.chunk(moment, which)
        z = Shifts(self.lanes)

        def tile(k, carry):
            start = pl.multiple_of(k * ROWS, ROWS)
            here = self.active(refs, moment, 1, start)
            xx = tile_reader(sh, 0, start)
            xy = tile_reader(sh, 1, start)
            xz = tile_reader(sh, 2, start)
            yy = tile_reader(so, 0, start)
            zz = tile_reader(so, 1, start)
            yz = tile_reader(so, 2, start)
            rows = pl.ds(start, ROWS)
            for i in range(self.cx):
                keep, gain = factors(here, refs["damp"][i, pl.ds(start, ROWS), :])
                gain = gain * refs["buoy"][i, pl.ds(start, ROWS), :]
                gx = fwd(lambda d: xx(i + 1 + d))
                gy = bwd(lambda d: xy(i + 2 + d))
                gz = bwd(lambda d: xz(i + 2 + d))
                if "inner" in refs:
                    gx = gx + refs["inner"][0, i, rows, :]
                    gy = gy + refs["inner"][1, i, rows, :]
                    gz = gz + refs["inner"][2, i, rows, :]
                else:
                    gx = gx + bwd(lambda d: xy(i + 2, d)) + z.bz(xz(i + 2))
                    gy = gy + fwd(lambda d: yy(i, d)) + z.bz(yz(i))
                    gz = gz + bwd(lambda d: yz(i, d)) + z.fz(zz(i))
                for f, g in enumerate((gx, gy, gz)):
                    refs["vel_next"][f, REACH + i, pl.ds(start + PAD, ROWS), :] = (
                        keep * previous(f, i, start) + gain * g
                    )
            return carry

        lax.fori_loop(first, last, tile, 0, unroll=True)
        odd = odd_slab()
        rows = pl.ds(PAD + first * ROWS, (last - first) * ROWS)
        for slot, (top, bottom, _, _) in enumerate(self.slots(moment)):
            field, layer = pick(odd, top[0], bottom[0]), pick(odd, top[1], bottom[1])
            refs["send_far"][slot] = refs["vel_next"][field, layer, rows, :]
            field, layer = pick(odd, bottom[0], top[0]), pick(odd, bottom[1], top[1])
            refs["send_near"][slot] = refs["vel_next"][field, layer, rows, :]

    def arrivals(self, refs, moment, which):
        first, last = self.chunk(moment, which)
        odd = odd_slab()
        rows = pl.ds(PAD + first * ROWS, (last - first) * ROWS)
        for slot, (_, _, below, above) in enumerate(self.slots(moment)):
            field, layer = pick(odd, above[0], below[0]), pick(odd, above[1], below[1])
            refs["vel"][field, layer, rows, :] = refs["from_far"][slot]
            field, layer = pick(odd, below[0], above[0]), pick(odd, below[1], above[1])
            refs["vel"][field, layer, rows, :] = refs["from_near"][slot]

    def stress_tiles(self, moment, which):
        first, last = self.chunk(moment, which)
        if which == 1:
            return first - 1, last
        return first, last - 1 if moment == self.steps - 1 else last

    def stress(self, refs, moment, which, final, part=None):
        first, last = part or self.stress_tiles(moment, which)
        base = self.stress_tiles(moment, which)[0]
        n = self.cx
        z = Shifts(self.lanes)
        old_h, old_o = refs["sh"], refs["so"]

        def tile(k, carry):
            start = pl.multiple_of(k * ROWS, ROWS)
            masks = [self.active(refs, moment, side, start) for side in range(3)]
            vx = tile_reader(refs["vel"], 0, start)
            vy = tile_reader(refs["vel"], 1, start)
            vz = tile_reader(refs["vel"], 2, start)
            rows = pl.ds(start, ROWS)
            padded = pl.ds(start + PAD, ROWS)

            def put_h(field, i, value):
                if final:
                    refs["done"][(0, 3, 4)[field], i, pl.ds(start - base * ROWS, ROWS), :] = value
                else:
                    refs["sh_next"][field, i + (1, 2, 2)[field], padded, :] = value

            def put_o(field, i, value):
                if final:
                    refs["done"][(1, 2, 5)[field], i, pl.ds(start - base * ROWS, ROWS), :] = value
                else:
                    refs["so_next"][field, i, padded, :] = value

            for i in range(0, n) if final else range(-2, n + 2):
                own = 0 <= i < n
                if own:
                    damp = refs["damp"][i, rows, :]
                else:
                    damp = refs["damp_edge"][i + 2 if i < 0 else i - n + 2, rows, :]
                keep, gain = factors(masks[0 if i < 0 else 1 if own else 2], damp)
                at = i + REACH
                mu = gain * refs["mu"][i + 2, rows, :]
                if i >= -1:
                    ex = bwd(lambda d: vx(at + d))
                    ey = bwd(lambda d: vy(at, d))
                    ez = z.bz(vz(at))
                    spread = gain * refs["lam"][i + 1, rows, :] * (ex + ey + ez)
                    mu2 = mu + mu
                    put_h(0, i, keep * old_h[0, i + 1, padded, :] + (spread + mu2 * ex))
                if own:
                    put_o(0, i, keep * old_o[0, i, padded, :] + (spread + mu2 * ey))
                    put_o(1, i, keep * old_o[1, i, padded, :] + (spread + mu2 * ez))
                    yz = z.fz(vy(at)) + fwd(lambda d: vz(at, d))
                    put_o(2, i, keep * old_o[2, i, padded, :] + mu * yz)
                if i <= n:
                    xy = fwd(lambda d: vx(at, d)) + fwd(lambda d: vy(at + d))
                    put_h(1, i, keep * old_h[1, i + 2, padded, :] + mu * xy)
                    xz = z.fz(vx(at)) + fwd(lambda d: vz(at + d))
                    put_h(2, i, keep * old_h[2, i + 2, padded, :] + mu * xz)
            return carry

        lax.fori_loop(first, last, tile, 0, unroll=True)

    def finish(self, refs, moment, which, done, sems):
        refs = dict(refs, done=done)
        first, last = self.stress_tiles(moment, which)
        copies = []

        def move(src, dst):
            copy = pltpu.make_async_copy(src, dst, sems.at[len(copies)])
            copy.start()
            copies.append(copy)

        for f in range(3):
            span = (last - first) * ROWS
            move(refs["vel"].at[f, pl.ds(REACH, self.cx), pl.ds(PAD + first * ROWS, span)],
                 refs["out"].at[0, f, :, pl.ds(first * ROWS, span)])
        for a, b in self.parts(first, last):
            self.stress(refs, moment, which, True, (a, b))
            span = (b - a) * ROWS
            for f in range(6):
                move(done.at[f, :, pl.ds((a - first) * ROWS, span)],
                     refs["out"].at[0, 3 + f, :, pl.ds(a * ROWS, span)])
        for copy in copies:
            copy.wait()

    @staticmethod
    def parts(first, last):
        middle = (first + last + 1) // 2
        return [(a, b) for a, b in ((first, middle), (middle, last)) if b > a]


STRESS_SLOTS = 5
MODEL_SLOTS = 6


def mover(sems):
    copies = []

    def move(src, dst):
        copy = pltpu.make_async_copy(src, dst, sems.at[len(copies)])
        copy.start()
        copies.append(copy)

    return move, copies


def pack_model(cx, refs, sems):
    odd = odd_slab()
    move, copies = mover(sems)
    for i, name in enumerate(("buoy", "q")):
        move(refs[name], refs["first"].at[pl.ds(i * cx, cx)])
    for i, name in enumerate(("lam", "mu", "q")):
        move(refs[name].at[pl.ds(pick(odd, cx - 2, 0), 2)], refs["edge"].at[pl.ds(2 * i, 2)])
    for i, name in enumerate(("lam", "mu")):
        move(refs[name], refs["second"].at[pl.ds(i * cx, cx)])
    for copy in copies:
        copy.wait()


def pack_stress(cx, refs, sems):
    odd = odd_slab()
    move, copies = mover(sems)
    top = [(3, cx - 1), (6, cx - 2), (6, cx - 1), (7, cx - 2), (7, cx - 1)]
    bottom = [(3, 0), (3, 1), (6, 0), (7, 0), (7, 0)]
    for name, flag in (("near", jnp.logical_not(odd)), ("far", odd)):
        for slot in range(STRESS_SLOTS):
            field = pick(flag, top[slot][0], bottom[slot][0])
            layer = pick(flag, top[slot][1], bottom[slot][1])
            move(refs["wave"].at[0, field, layer], refs[name].at[slot])
    for copy in copies:
        copy.wait()


def prepare(plan, refs):
    cx, rows = plan.cx, plan.rows
    zero_pads(refs["sh"], rows)
    zero_pads(refs["so"], rows)
    inner = pl.ds(PAD, rows)
    for field, (source, shift) in enumerate(((3, 1), (6, 2), (7, 2))):
        for i in range(cx):
            refs["sh"][field, i + shift, inner, :] = refs["wave"][0, source, i]
    for field, source in enumerate((4, 5, 8)):
        for i in range(cx):
            refs["so"][field, i, inner, :] = refs["wave"][0, source, i]
    for field in range(3):
        for i in range(cx):
            refs["old"][field, i] = refs["wave"][0, field, i]
    plan.inner_forcing(refs, refs["sh"], refs["so"])
    lane_blocks = refs["active"].shape[1]
    block = lax.broadcasted_iota(jnp.int32, (lane_blocks, plan.lanes), 1) // (plan.lanes // lane_blocks)
    own = block == lax.broadcasted_iota(jnp.int32, (lane_blocks, plan.lanes), 0)
    refs["mask"][...] = jnp.dot(refs["active"][...].astype(F32), own.astype(F32),
                                preferred_element_type=F32)


def hold(array, *others):
    return call(lambda refs: None, dict(array=array), dict(array=array.shape), alias=("array",),
                us=0.02, waits=others)["array"]


def spread(mine, shots):
    pairs = lambda k: [(i, i ^ k) for i in range(shots)]
    if shots == 4:
        beside = lax.ppermute(mine, "shot", pairs(1))
        across = lax.ppermute(mine, "shot", pairs(2))

        def finish(*others):
            handed = lax.ppermute(hold(across, beside, *others), "shot", pairs(1))
            return {0: mine, 1: beside, 2: across, 3: handed}

        return (beside, across), finish
    turn = lambda k: [(i, (i + k) % shots) for i in range(shots)]
    swap = shots & (shots - 1) == 0
    got = {k: lax.ppermute(mine, "shot", pairs(k) if swap else turn(k)) for k in range(1, shots)}
    return tuple(got.values()), lambda *others: {0: mine, **got}


def origin_of(index, k, shots):
    if shots & (shots - 1) == 0:
        return index ^ k
    return lax.rem(index + shots - k, shots)


def panel_place(k, shots, panel_rows):
    start = origin_of(lax.axis_index("shot"), k, shots) * panel_rows
    return pl.ds(pl.multiple_of(start, panel_rows), panel_rows)


def per_device(cuts_of, shots, slabs, wave, lam, mu, buoy, q, active):
    cx, panel_rows, lanes = lam.shape
    rows = wave.shape[3]
    steps, _, blocks, lane_blocks = active.shape
    plan = Plan(cx, rows, lanes, blocks, steps, slabs, cuts_of(steps, rows // ROWS))
    padded = rows + 2 * PAD
    far = [(i, i + 1) for i in range(1, slabs - 1, 2)]
    near = [(i, i + 1) for i in range(0, slabs - 1, 2)]
    far = far + [(j, i) for i, j in far]
    near = near + [(j, i) for i, j in near]

    def exchange(to_far, to_near):
        return lax.ppermute(to_far, "aper", far), lax.ppermute(to_near, "aper", near)

    panel = (panel_rows, lanes)
    sent = call(
        functools.partial(pack_model, cx), dict(lam=lam, mu=mu, buoy=buoy, q=q),
        dict(first=(2 * cx,) + panel, second=(2 * cx,) + panel, edge=(MODEL_SLOTS,) + panel),
        scratch=[pltpu.SemaphoreType.DMA((7,))], anywhere=("lam", "mu", "buoy", "q"), us=0.02,
    )
    edge = lax.ppermute(sent["edge"], "aper", far)
    sent.update(call(
        functools.partial(pack_stress, cx), dict(wave=wave),
        dict(far=(STRESS_SLOTS, rows, lanes), near=(STRESS_SLOTS, rows, lanes)),
        scratch=[pltpu.SemaphoreType.DMA((2 * STRESS_SLOTS,))], anywhere=("wave",), us=5.0, waits=(edge,),
    ))
    halo_far, halo_near = exchange(sent["far"], sent["near"])
    sh_shape, so_shape = (3, cx + 3, padded, lanes), (3, cx, padded, lanes)
    vel_shape, slab_shape = (3, cx + 2 * REACH, padded, lanes), (cx, rows, lanes)
    state = call(functools.partial(prepare, plan), dict(wave=wave, active=active.reshape(-1, lane_blocks)),
                 dict(sh=sh_shape, so=so_shape, old=(3,) + slab_shape, inner=(3,) + slab_shape, mask=(steps * slabs * blocks, lanes)), us=5.0)

    first_stage, finish = spread(sent["first"], shots)
    mask = state["mask"]
    firsts = finish(edge)

    def join(refs):
        refs["all"][:2 * cx] = refs["second"][...]
        refs["all"][2 * cx:] = refs["edge"][...]

    second = call(join, dict(second=sent["second"], edge=edge),
                  dict(all=(2 * cx + MODEL_SLOTS,) + panel), us=0.02, waits=first_stage + (mask,))["all"]
    _, finish_second = spread(second, shots)

    def sends(step, which):
        first, last = plan.chunk(step, which)
        shape = (len(plan.slots(step)), (last - first) * ROWS, lanes)
        return dict(send_far=shape, send_near=shape)

    def start_first(refs):
        odd = odd_slab()
        inner = pl.ds(PAD, rows)
        below = [(0, 0), (1, 0), (1, 1), (2, 0), (2, 1)]
        above = [(0, cx + 1), (0, cx + 2), (1, cx + 2), (2, cx + 2), (2, cx + 2)]
        for slot in range(STRESS_SLOTS):
            field = pick(odd, above[slot][0], below[slot][0])
            layer = pick(odd, above[slot][1], below[slot][1])
            refs["sh"][field, layer, inner, :] = refs["halo_far"][slot]
            field = pick(odd, below[slot][0], above[slot][0])
            layer = pick(odd, below[slot][1], above[slot][1])
            refs["sh"][field, layer, inner, :] = refs["halo_near"][slot]
        for k in firsts:
            place, got = panel_place(k, shots, panel_rows), refs["first%d" % k]
            for i in range(cx):
                refs["buoy"][i, place, :] = got[i]
                refs["damp"][i, place, :] = jnp.exp(-DT * got[cx + i])
        zero_pads(refs["vel_next"], rows)
        start_chunk(refs, 0)

    def start_chunk(refs, which):
        plan.velocity(refs, 0, which, refs["sh"], refs["so"],
                      lambda f, i, start: refs["old"][f, i, pl.ds(start, ROWS), :])

    ins = dict(halo_far=halo_far, halo_near=halo_near, **state)
    ins.update({"first%d" % k: a for k, a in firsts.items()})
    got = call(start_first, ins,
               dict(sh=sh_shape, buoy=slab_shape, damp=slab_shape, vel_next=vel_shape,
                    **sends(0, 0)),
               alias=("sh",), us=1.2)
    sh, so = got["sh"], state["so"]
    model = dict(mask=mask, buoy=got["buoy"], damp=got["damp"])
    arrived = [exchange(got["send_far"], got["send_near"])]
    got = call(lambda refs: start_chunk(refs, 1),
               dict(sh=sh, so=so, old=state["old"], inner=state["inner"], vel_next=got["vel_next"], **model),
               dict(vel_next=vel_shape, **sends(0, 1)), alias=("vel_next",), us=0.8)
    vel = got["vel_next"]
    arrived.append(exchange(got["send_far"], got["send_near"]))

    seconds = finish_second()

    def put_edge(refs, from_above, place, part):
        for j in range(2):
            refs["lam"][pick(from_above, cx + 1 + j, 0), place, :] = part(j)
            refs["mu"][pick(from_above, cx + 2 + j, j), place, :] = part(2 + j)
            refs["damp_edge"][pick(from_above, 2 + j, j), place, :] = part(4 + j)

    def assemble(refs):
        odd = odd_slab()
        for k in seconds:
            place, got = panel_place(k, shots, panel_rows), refs["second%d" % k]
            for i in range(cx):
                refs["lam"][i + 1, place, :] = got[i]
                refs["mu"][i + 2, place, :] = got[cx + i]
            put_edge(refs, odd, place, lambda slot: jnp.exp(-DT * got[2 * cx + slot])
                     if slot >= 4 else got[2 * cx + slot])
        for j in range(2):
            at = pick(odd, j, cx - 2 + j)
            refs["send_model"][j] = refs["lam"][at + 1]
            refs["send_model"][2 + j] = refs["mu"][at + 2]
            refs["send_model"][4 + j] = refs["damp"][at]

    edges = dict(lam=(cx + 3, rows, lanes), mu=(cx + 4, rows, lanes), damp_edge=(4, rows, lanes))
    got = call(assemble, dict(damp=model["damp"], **{"second%d" % k: a for k, a in seconds.items()}),
               dict(send_model=(MODEL_SLOTS, rows, lanes), **edges), us=0.02, waits=(arrived[1][1],))
    model_near = lax.ppermute(got["send_model"], "aper", near)
    model.update({name: got[name] for name in edges})
    vel = call(lambda refs: plan.arrivals(refs, 0, 0),
               dict(vel=vel, from_far=arrived[0][0], from_near=arrived[0][1]),
               dict(vel=vel_shape), alias=("vel",), us=20.0)["vel"]

    out_shape = wave.shape
    for step in range(steps):
        final = step == steps - 1

        def advance(refs, *scratch, which, step=step, final=final):
            if step == 0 and which == 0:
                put_edge(refs, jnp.logical_not(odd_slab()), slice(None), lambda slot: refs["model_near"][slot])
            else:
                plan.arrivals(refs, step, which)
            if final:
                plan.finish(refs, step, which, *scratch)
                return
            if which == 0:
                zero_pads(refs["sh_next"], rows)
                zero_pads(refs["so_next"], rows)
                zero_pads(refs["vel_next"], rows)
            plan.stress(refs, step, which, False)
            plan.velocity(
                refs, step + 1, which, refs["sh_next"], refs["so_next"],
                lambda f, i, start: refs["vel"][f, REACH + i, pl.ds(start + PAD, ROWS), :])

        nexts = dict(out=out_shape) if final else dict(
            sh_next=sh_shape, so_next=so_shape, vel_next=vel_shape)
        following = []
        carried = {}
        for which in range(2):
            ins = dict(vel=vel, sh=sh, so=so, from_far=arrived[which][0], from_near=arrived[which][1],
                       **model, **carried)
            outs = dict(vel=vel_shape, **nexts)
            if step == 0 and which == 0:
                ins.update(model_near=model_near)
                outs.update(edges)
            scratch = []
            if final:
                first, last = plan.stress_tiles(step, which)
                scratch = [pltpu.VMEM((6, cx, (last - first) * ROWS, lanes), F32),
                           pltpu.SemaphoreType.DMA((3 + 6 * len(plan.parts(first, last)),))]
            else:
                outs.update(sends(step + 1, which))
            got = call(functools.partial(advance, which=which), ins, outs, alias=("vel",) + tuple(carried) + (tuple(edges) if step + which == 0 else ()),
                       scratch=scratch, anywhere=("out",))
            vel = got["vel"]
            if step == 0 and which == 0:
                model.update({name: got[name] for name in edges})
            carried = {name: got[name] for name in nexts}
            if not final:
                following.append(exchange(got["send_far"], got["send_near"]))
        if final:
            return carried["out"]
        vel, sh, so, arrived = carried["vel_next"], carried["sh_next"], carried["so_next"], following


def cuts_of(steps, tiles):
    middle = tiles // 2 + 1
    return [max(1, middle - step) for step in range(steps)]


def solution(mesh):
    body = functools.partial(per_device, cuts_of, mesh.shape["shot"], mesh.shape["aper"])
    return jax.shard_map(
        body,
        mesh=mesh,
        in_specs=(
            P("shot", None, "aper", None, None),
            P("aper", "shot", None),
            P("aper", "shot", None),
            P("aper", "shot", None),
            P("aper", "shot", None),
            P(),
        ),
        out_specs=P("shot", None, "aper", None, None),
        check_vma=False,
    )
```

```python
import functools

import jax
import jax.numpy as jnp
from jax import lax
from jax.experimental import pallas as pl
from jax.experimental.pallas import tpu as pltpu
from jax.sharding import PartitionSpec as P

NEAR = 1.125
FAR = -1.0 / 24.0
RATIO = FAR / NEAR
DT = 0.2
ROWS = 8
PAD = 8
REACH = 3
VMEM = pl.BlockSpec(memory_space=pltpu.VMEM)
ANY = pl.BlockSpec(memory_space=pl.ANY)
F32 = jnp.float32


def call(body, ins, outs, alias=(), scratch=(), anywhere=(), us=5.0, waits=()):
    ins = dict(ins, **{"wait%d" % i: a for i, a in enumerate(waits)})
    in_names, out_names = list(ins), list(outs)

    def kernel(*refs):
        names = {}
        for name, ref in zip(in_names, refs):
            if name not in alias:
                names[name] = ref
        for name, ref in zip(out_names, refs[len(in_names):]):
            names[name] = ref
        body(names, *refs[len(in_names) + len(out_names):])

    ins = {name: pltpu.with_memory_space_constraint(a, pltpu.HBM) if name in anywhere
           else pltpu.with_memory_space_constraint(a, pltpu.VMEM) if name in alias
           else a for name, a in ins.items()}
    results = pl.pallas_call(
        kernel,
        out_shape=[pltpu.HBM(shape, F32) if name in anywhere else pltpu.VMEM(shape, F32)
                   for name, shape in outs.items()],
        in_specs=[ANY if name in anywhere or name[:4] == "wait" else VMEM for name in in_names],
        out_specs=[ANY if name in anywhere else VMEM for name in out_names],
        scratch_shapes=list(scratch),
        input_output_aliases={in_names.index(n): out_names.index(n) for n in alias},
        compiler_params=pltpu.CompilerParams(vmem_limit_bytes=24 * 2**20),
        cost_estimate=pl.CostEstimate(flops=int(us * 1e9), bytes_accessed=int(us * 3.6e6), transcendentals=0),
    )(*ins.values())
    return dict(zip(out_names, results))


def odd_slab():
    return lax.rem(lax.axis_index("aper"), 2) == 1


def pick(flag, yes, no):
    return jnp.where(flag, jnp.int32(yes), jnp.int32(no))


class Shifts:
    def __init__(self, lanes):
        lane = lax.broadcasted_iota(jnp.int32, (ROWS, lanes), 1)
        self.lanes = lanes
        self.f_up1 = jnp.where(lane < lanes - 1, F32(1), F32(0))
        self.f_up2 = jnp.where(lane < lanes - 2, F32(RATIO), F32(0))
        self.f_dn1 = jnp.where(lane >= 1, F32(RATIO), F32(0))
        self.b_dn1 = jnp.where(lane >= 1, F32(1), F32(0))
        self.b_dn2 = jnp.where(lane >= 2, F32(RATIO), F32(0))
        self.b_up1 = jnp.where(lane < lanes - 1, F32(RATIO), F32(0))

    def fz(self, f):
        n = self.lanes
        return (self.f_up1 * pltpu.roll(f, n - 1, 1) - f) + (
            self.f_up2 * pltpu.roll(f, n - 2, 1) - self.f_dn1 * pltpu.roll(f, 1, 1)
        )

    def bz(self, f):
        n = self.lanes
        return (f - self.b_dn1 * pltpu.roll(f, 1, 1)) + (
            self.b_up1 * pltpu.roll(f, n - 1, 1) - self.b_dn2 * pltpu.roll(f, 2, 1)
        )


def fwd(at):
    return (at(1) - at(0)) + RATIO * (at(2) - at(-1))


def bwd(at):
    return (at(0) - at(-1)) + RATIO * (at(1) - at(-2))


def tile_reader(ref, field, start):
    seen = {}

    def read(layer, dy=0):
        if (layer, dy) not in seen:
            seen[layer, dy] = ref[field, layer, pl.ds(start + PAD + dy, ROWS), :]
        return seen[layer, dy]

    return read


def factors(active_cells, damp):
    return jnp.where(active_cells, damp, F32(1)), jnp.where(active_cells, (DT * NEAR) * damp, F32(0))


def zero_pads(ref, rows):
    zeros = jnp.zeros((ref.shape[0], ref.shape[1], PAD, ref.shape[3]), F32)
    ref[:, :, :PAD, :] = zeros
    ref[:, :, PAD + rows:, :] = zeros


class Plan:
    def __init__(self, cx, rows, lanes, blocks, steps, slabs, cuts):
        self.slabs = slabs
        self.cx, self.rows, self.lanes = cx, rows, lanes
        self.blocks, self.steps, self.cuts = blocks, steps, cuts
        self.block_rows = rows // blocks
        self.tiles = rows // ROWS

    def active(self, refs, moment, side, start):
        slab = jnp.clip(lax.axis_index("aper") + side - 1, 0, self.slabs - 1)
        row = (moment * self.slabs + slab) * self.blocks + start // self.block_rows
        return jnp.broadcast_to(refs["mask"][pl.ds(row, 1), :], (ROWS, self.lanes)) > 0

    def chunk(self, step, which):
        cut = self.cuts[step]
        return (0, cut) if which == 0 else (cut, self.tiles)

    def slots(self, step):
        n = self.cx
        if step < self.steps - 1:
            return [
                ((f, n + j), (f, REACH + j), (f, j), (f, n + REACH + j))
                for f in range(3) for j in range(REACH)
            ]
        top = [(0, n + 1), (0, n + 2), (1, n + 2), (2, n + 2), (2, n + 2)]
        bottom = [(0, 3), (1, 4), (1, 3), (2, 3), (2, 4)]
        below = [(0, 1), (0, 2), (1, 2), (2, 2), (2, 2)]
        above = [(0, n + 3), (1, n + 4), (1, n + 3), (2, n + 3), (2, n + 4)]
        return list(zip(top, bottom, below, above))

    def inner_forcing(self, refs, sh, so):
        z = Shifts(self.lanes)

        def tile(k, carry):
            start = pl.multiple_of(k * ROWS, ROWS)
            rows = pl.ds(start, ROWS)
            xy = tile_reader(sh, 1, start)
            xz = tile_reader(sh, 2, start)
            yy = tile_reader(so, 0, start)
            zz = tile_reader(so, 1, start)
            yz = tile_reader(so, 2, start)
            for i in range(self.cx):
                refs["inner"][0, i, rows, :] = bwd(lambda d: xy(i + 2, d)) + z.bz(xz(i + 2))
                refs["inner"][1, i, rows, :] = fwd(lambda d: yy(i, d)) + z.bz(yz(i))
                refs["inner"][2, i, rows, :] = bwd(lambda d: yz(i, d)) + z.fz(zz(i))
            return carry

        lax.fori_loop(0, self.tiles, tile, 0)

    def velocity(self, refs, moment, which, sh, so, previous):
        first, last = self.chunk(moment, which)
        z = Shifts(self.lanes)

        def tile(k, carry):
            start = pl.multiple_of(k * ROWS, ROWS)
            here = self.active(refs, moment, 1, start)
            xx = tile_reader(sh, 0, start)
            xy = tile_reader(sh, 1, start)
            xz = tile_reader(sh, 2, start)
            yy = tile_reader(so, 0, start)
            zz = tile_reader(so, 1, start)
            yz = tile_reader(so, 2, start)
            rows = pl.ds(start, ROWS)
            for i in range(self.cx):
                keep, gain = factors(here, refs["damp"][i, pl.ds(start, ROWS), :])
                gain = gain * refs["buoy"][i, pl.ds(start, ROWS), :]
                gx = fwd(lambda d: xx(i + 1 + d))
                gy = bwd(lambda d: xy(i + 2 + d))
                gz = bwd(lambda d: xz(i + 2 + d))
                if "inner" in refs:
                    gx = gx + refs["inner"][0, i, rows, :]
                    gy = gy + refs["inner"][1, i, rows, :]
                    gz = gz + refs["inner"][2, i, rows, :]
                else:
                    gx = gx + bwd(lambda d: xy(i + 2, d)) + z.bz(xz(i + 2))
                    gy = gy + fwd(lambda d: yy(i, d)) + z.bz(yz(i))
                    gz = gz + bwd(lambda d: yz(i, d)) + z.fz(zz(i))
                for f, g in enumerate((gx, gy, gz)):
                    refs["vel_next"][f, REACH + i, pl.ds(start + PAD, ROWS), :] = (
                        keep * previous(f, i, start) + gain * g
                    )
            return carry

        lax.fori_loop(first, last, tile, 0, unroll=True)
        odd = odd_slab()
        rows = pl.ds(PAD + first * ROWS, (last - first) * ROWS)
        for slot, (top, bottom, _, _) in enumerate(self.slots(moment)):
            field, layer = pick(odd, top[0], bottom[0]), pick(odd, top[1], bottom[1])
            refs["send_far"][slot] = refs["vel_next"][field, layer, rows, :]
            field, layer = pick(odd, bottom[0], top[0]), pick(odd, bottom[1], top[1])
            refs["send_near"][slot] = refs["vel_next"][field, layer, rows, :]

    def arrivals(self, refs, moment, which):
        first, last = self.chunk(moment, which)
        odd = odd_slab()
        rows = pl.ds(PAD + first * ROWS, (last - first) * ROWS)
        for slot, (_, _, below, above) in enumerate(self.slots(moment)):
            field, layer = pick(odd, above[0], below[0]), pick(odd, above[1], below[1])
            refs["vel"][field, layer, rows, :] = refs["from_far"][slot]
            field, layer = pick(odd, below[0], above[0]), pick(odd, below[1], above[1])
            refs["vel"][field, layer, rows, :] = refs["from_near"][slot]

    def stress_tiles(self, moment, which):
        first, last = self.chunk(moment, which)
        if which == 1:
            return first - 1, last
        return first, last - 1 if moment == self.steps - 1 else last

    def stress(self, refs, moment, which, final, part=None):
        first, last = part or self.stress_tiles(moment, which)
        base = self.stress_tiles(moment, which)[0]
        n = self.cx
        z = Shifts(self.lanes)
        old_h, old_o = refs["sh"], refs["so"]

        def tile(k, carry):
            start = pl.multiple_of(k * ROWS, ROWS)
            masks = [self.active(refs, moment, side, start) for side in range(3)]
            vx = tile_reader(refs["vel"], 0, start)
            vy = tile_reader(refs["vel"], 1, start)
            vz = tile_reader(refs["vel"], 2, start)
            rows = pl.ds(start, ROWS)
            padded = pl.ds(start + PAD, ROWS)

            def put_h(field, i, value):
                if final:
                    refs["done"][(0, 3, 4)[field], i, pl.ds(start - base * ROWS, ROWS), :] = value
                else:
                    refs["sh_next"][field, i + (1, 2, 2)[field], padded, :] = value

            def put_o(field, i, value):
                if final:
                    refs["done"][(1, 2, 5)[field], i, pl.ds(start - base * ROWS, ROWS), :] = value
                else:
                    refs["so_next"][field, i, padded, :] = value

            for i in range(0, n) if final else range(-2, n + 2):
                own = 0 <= i < n
                if own:
                    damp = refs["damp"][i, rows, :]
                else:
                    damp = refs["damp_edge"][i + 2 if i < 0 else i - n + 2, rows, :]
                keep, gain = factors(masks[0 if i < 0 else 1 if own else 2], damp)
                at = i + REACH
                mu = gain * refs["mu"][i + 2, rows, :]
                if i >= -1:
                    ex = bwd(lambda d: vx(at + d))
                    ey = bwd(lambda d: vy(at, d))
                    ez = z.bz(vz(at))
                    spread = gain * refs["lam"][i + 1, rows, :] * (ex + ey + ez)
                    mu2 = mu + mu
                    put_h(0, i, keep * old_h[0, i + 1, padded, :] + (spread + mu2 * ex))
                if own:
                    put_o(0, i, keep * old_o[0, i, padded, :] + (spread + mu2 * ey))
                    put_o(1, i, keep * old_o[1, i, padded, :] + (spread + mu2 * ez))
                    yz = z.fz(vy(at)) + fwd(lambda d: vz(at, d))
                    put_o(2, i, keep * old_o[2, i, padded, :] + mu * yz)
                if i <= n:
                    xy = fwd(lambda d: vx(at, d)) + fwd(lambda d: vy(at + d))
                    put_h(1, i, keep * old_h[1, i + 2, padded, :] + mu * xy)
                    xz = z.fz(vx(at)) + fwd(lambda d: vz(at + d))
                    put_h(2, i, keep * old_h[2, i + 2, padded, :] + mu * xz)
            return carry

        lax.fori_loop(first, last, tile, 0, unroll=True)

    def finish(self, refs, moment, which, done, sems):
        refs = dict(refs, done=done)
        first, last = self.stress_tiles(moment, which)
        copies = []

        def move(src, dst):
            copy = pltpu.make_async_copy(src, dst, sems.at[len(copies)])
            copy.start()
            copies.append(copy)

        if which == 0:
            for f in range(3):
                move(refs["vel"].at[f, pl.ds(REACH, self.cx), pl.ds(PAD, self.rows)], refs["out"].at[0, f])
        for a, b in self.parts(first, last):
            self.stress(refs, moment, which, True, (a, b))
            span = (b - a) * ROWS
            for f in range(6):
                move(done.at[f, :, pl.ds((a - first) * ROWS, span)],
                     refs["out"].at[0, 3 + f, :, pl.ds(a * ROWS, span)])
        for copy in copies:
            copy.wait()

    @staticmethod
    def parts(first, last):
        marks = [first, (first + last) // 2, last - (last - first) // 5, last]
        return [(a, b) for a, b in zip(marks, marks[1:]) if b > a]


STRESS_SLOTS = 5
MODEL_SLOTS = 6


def mover(sems):
    copies = []

    def move(src, dst):
        copy = pltpu.make_async_copy(src, dst, sems.at[len(copies)])
        copy.start()
        copies.append(copy)

    return move, copies


def pack_model(cx, refs, sems):
    odd = odd_slab()
    move, copies = mover(sems)
    for i, name in enumerate(("buoy", "q")):
        move(refs[name], refs["first"].at[pl.ds(i * cx, cx)])
    for i, name in enumerate(("lam", "mu", "q")):
        move(refs[name].at[pl.ds(pick(odd, cx - 2, 0), 2)], refs["edge"].at[pl.ds(2 * i, 2)])
    for i, name in enumerate(("lam", "mu")):
        move(refs[name], refs["second"].at[pl.ds(i * cx, cx)])
    for copy in copies:
        copy.wait()


def pack_stress(cx, refs, sems):
    odd = odd_slab()
    move, copies = mover(sems)
    top = [(3, cx - 1), (6, cx - 2), (6, cx - 1), (7, cx - 2), (7, cx - 1)]
    bottom = [(3, 0), (3, 1), (6, 0), (7, 0), (7, 0)]
    for name, flag in (("near", jnp.logical_not(odd)), ("far", odd)):
        for slot in range(STRESS_SLOTS):
            field = pick(flag, top[slot][0], bottom[slot][0])
            layer = pick(flag, top[slot][1], bottom[slot][1])
            move(refs["wave"].at[0, field, layer], refs[name].at[slot])
    for copy in copies:
        copy.wait()


def prepare(plan, refs):
    cx, rows = plan.cx, plan.rows
    zero_pads(refs["sh"], rows)
    zero_pads(refs["so"], rows)
    inner = pl.ds(PAD, rows)
    for field, (source, shift) in enumerate(((3, 1), (6, 2), (7, 2))):
        for i in range(cx):
            refs["sh"][field, i + shift, inner, :] = refs["wave"][0, source, i]
    for field, source in enumerate((4, 5, 8)):
        for i in range(cx):
            refs["so"][field, i, inner, :] = refs["wave"][0, source, i]
    for field in range(3):
        for i in range(cx):
            refs["old"][field, i] = refs["wave"][0, field, i]
    plan.inner_forcing(refs, refs["sh"], refs["so"])
    lane_blocks = refs["active"].shape[1]
    block = lax.broadcasted_iota(jnp.int32, (lane_blocks, plan.lanes), 1) // (plan.lanes // lane_blocks)
    own = block == lax.broadcasted_iota(jnp.int32, (lane_blocks, plan.lanes), 0)
    refs["mask"][...] = jnp.dot(refs["active"][...].astype(F32), own.astype(F32),
                                preferred_element_type=F32)


def hold(array, *others):
    return call(lambda refs: None, dict(array=array), dict(array=array.shape), alias=("array",),
                us=0.02, waits=others)["array"]


def spread(mine, shots):
    pairs = lambda k: [(i, i ^ k) for i in range(shots)]
    if shots == 4:
        beside = lax.ppermute(mine, "shot", pairs(1))
        across = lax.ppermute(mine, "shot", pairs(2))

        def finish(*others):
            held = hold(across, beside, *others)
            handed = lax.ppermute(held, "shot", pairs(1))
            return {0: mine, 1: beside, 2: across, 3: handed}, held

        return (beside, across), finish
    turn = lambda k: [(i, (i + k) % shots) for i in range(shots)]
    swap = shots & (shots - 1) == 0
    got = {k: lax.ppermute(mine, "shot", pairs(k) if swap else turn(k)) for k in range(1, shots)}
    return tuple(got.values()), lambda *others: ({0: mine, **got}, mine)


def origin_of(index, k, shots):
    if shots & (shots - 1) == 0:
        return index ^ k
    return lax.rem(index + shots - k, shots)


def panel_place(k, shots, panel_rows):
    start = origin_of(lax.axis_index("shot"), k, shots) * panel_rows
    return pl.ds(pl.multiple_of(start, panel_rows), panel_rows)


def per_device(cuts_of, shots, slabs, wave, lam, mu, buoy, q, active):
    cx, panel_rows, lanes = lam.shape
    rows = wave.shape[3]
    steps, _, blocks, lane_blocks = active.shape
    plan = Plan(cx, rows, lanes, blocks, steps, slabs, cuts_of(steps, rows // ROWS))
    padded = rows + 2 * PAD
    far = [(i, i + 1) for i in range(1, slabs - 1, 2)]
    near = [(i, i + 1) for i in range(0, slabs - 1, 2)]
    far = far + [(j, i) for i, j in far]
    near = near + [(j, i) for i, j in near]

    def exchange(to_far, to_near):
        return lax.ppermute(to_far, "aper", far), lax.ppermute(to_near, "aper", near)

    panel = (panel_rows, lanes)
    sent = call(
        functools.partial(pack_model, cx), dict(lam=lam, mu=mu, buoy=buoy, q=q),
        dict(first=(2 * cx,) + panel, second=(2 * cx,) + panel, edge=(MODEL_SLOTS,) + panel),
        scratch=[pltpu.SemaphoreType.DMA((7,))], anywhere=("lam", "mu", "buoy", "q"), us=0.02,
    )
    edge = lax.ppermute(sent["edge"], "aper", far)
    sent.update(call(
        functools.partial(pack_stress, cx), dict(wave=wave),
        dict(far=(STRESS_SLOTS, rows, lanes), near=(STRESS_SLOTS, rows, lanes)),
        scratch=[pltpu.SemaphoreType.DMA((2 * STRESS_SLOTS,))], anywhere=("wave",), us=5.0, waits=(edge,),
    ))
    halo_far, halo_near = exchange(sent["far"], sent["near"])
    sh_shape, so_shape = (3, cx + 3, padded, lanes), (3, cx, padded, lanes)
    vel_shape, slab_shape = (3, cx + 2 * REACH, padded, lanes), (cx, rows, lanes)
    state = call(functools.partial(prepare, plan), dict(wave=wave, active=active.reshape(-1, lane_blocks)),
                 dict(sh=sh_shape, so=so_shape, old=(3,) + slab_shape, inner=(3,) + slab_shape, mask=(steps * slabs * blocks, lanes)), us=5.0)

    first_stage, finish = spread(sent["first"], shots)
    mask = state["mask"]
    firsts, held = finish(edge)

    def mark(refs):
        refs["tick"][...] = jnp.zeros(refs["tick"].shape, F32)

    tick = call(mark, {}, dict(tick=(ROWS, lanes)), waits=(held,))["tick"]

    def join(refs):
        refs["all"][:2 * cx] = refs["second"][...]
        refs["all"][2 * cx:] = refs["edge"][...]

    second = call(join, dict(second=sent["second"], edge=edge),
                  dict(all=(2 * cx + MODEL_SLOTS,) + panel), us=0.02, waits=first_stage + (tick,))["all"]
    _, finish_second = spread(second, shots)

    def sends(step, which):
        first, last = plan.chunk(step, which)
        shape = (len(plan.slots(step)), (last - first) * ROWS, lanes)
        return dict(send_far=shape, send_near=shape)

    def start_first(refs):
        odd = odd_slab()
        inner = pl.ds(PAD, rows)
        below = [(0, 0), (1, 0), (1, 1), (2, 0), (2, 1)]
        above = [(0, cx + 1), (0, cx + 2), (1, cx + 2), (2, cx + 2), (2, cx + 2)]
        for slot in range(STRESS_SLOTS):
            field = pick(odd, above[slot][0], below[slot][0])
            layer = pick(odd, above[slot][1], below[slot][1])
            refs["sh"][field, layer, inner, :] = refs["halo_far"][slot]
            field = pick(odd, below[slot][0], above[slot][0])
            layer = pick(odd, below[slot][1], above[slot][1])
            refs["sh"][field, layer, inner, :] = refs["halo_near"][slot]
        for k in firsts:
            place, got = panel_place(k, shots, panel_rows), refs["first%d" % k]
            for i in range(cx):
                refs["buoy"][i, place, :] = got[i]
                refs["damp"][i, place, :] = jnp.exp(-DT * got[cx + i])
        zero_pads(refs["vel_next"], rows)
        start_chunk(refs, 0)

    def start_chunk(refs, which):
        plan.velocity(refs, 0, which, refs["sh"], refs["so"],
                      lambda f, i, start: refs["old"][f, i, pl.ds(start, ROWS), :])

    ins = dict(halo_far=halo_far, halo_near=halo_near, **state)
    ins.update({"first%d" % k: a for k, a in firsts.items()})
    got = call(start_first, ins,
               dict(sh=sh_shape, buoy=slab_shape, damp=slab_shape, vel_next=vel_shape,
                    **sends(0, 0)),
               alias=("sh",), us=1.2)
    sh, so = got["sh"], state["so"]
    model = dict(mask=mask, buoy=got["buoy"], damp=got["damp"])
    arrived = [exchange(got["send_far"], got["send_near"])]
    got = call(lambda refs: start_chunk(refs, 1),
               dict(sh=sh, so=so, old=state["old"], inner=state["inner"], vel_next=got["vel_next"], **model),
               dict(vel_next=vel_shape, **sends(0, 1)), alias=("vel_next",), us=0.8)
    vel = got["vel_next"]
    arrived.append(exchange(got["send_far"], got["send_near"]))

    seconds, _ = finish_second()

    def put_edge(refs, from_above, place, part):
        for j in range(2):
            refs["lam"][pick(from_above, cx + 1 + j, 0), place, :] = part(j)
            refs["mu"][pick(from_above, cx + 2 + j, j), place, :] = part(2 + j)
            refs["damp_edge"][pick(from_above, 2 + j, j), place, :] = part(4 + j)

    def assemble(refs):
        odd = odd_slab()
        for k in seconds:
            place, got = panel_place(k, shots, panel_rows), refs["second%d" % k]
            for i in range(cx):
                refs["lam"][i + 1, place, :] = got[i]
                refs["mu"][i + 2, place, :] = got[cx + i]
            put_edge(refs, odd, place, lambda slot: jnp.exp(-DT * got[2 * cx + slot])
                     if slot >= 4 else got[2 * cx + slot])
        for j in range(2):
            at = pick(odd, j, cx - 2 + j)
            refs["send_model"][j] = refs["lam"][at + 1]
            refs["send_model"][2 + j] = refs["mu"][at + 2]
            refs["send_model"][4 + j] = refs["damp"][at]

    edges = dict(lam=(cx + 3, rows, lanes), mu=(cx + 4, rows, lanes), damp_edge=(4, rows, lanes))
    got = call(assemble, dict(damp=model["damp"], **{"second%d" % k: a for k, a in seconds.items()}),
               dict(send_model=(MODEL_SLOTS, rows, lanes), **edges), us=0.02, waits=(arrived[1][1],))
    model_near = lax.ppermute(got["send_model"], "aper", near)
    model.update({name: got[name] for name in edges})
    vel = call(lambda refs: plan.arrivals(refs, 0, 0),
               dict(vel=vel, from_far=arrived[0][0], from_near=arrived[0][1]),
               dict(vel=vel_shape), alias=("vel",), us=20.0)["vel"]

    out_shape = wave.shape
    for step in range(steps):
        final = step == steps - 1

        def advance(refs, *scratch, which, step=step, final=final):
            if step == 0 and which == 0:
                put_edge(refs, jnp.logical_not(odd_slab()), slice(None), lambda slot: refs["model_near"][slot])
            else:
                plan.arrivals(refs, step, which)
            if final:
                plan.finish(refs, step, which, *scratch)
                return
            if which == 0:
                zero_pads(refs["sh_next"], rows)
                zero_pads(refs["so_next"], rows)
                zero_pads(refs["vel_next"], rows)
            plan.stress(refs, step, which, False)
            plan.velocity(
                refs, step + 1, which, refs["sh_next"], refs["so_next"],
                lambda f, i, start: refs["vel"][f, REACH + i, pl.ds(start + PAD, ROWS), :])

        nexts = dict(out=out_shape) if final else dict(
            sh_next=sh_shape, so_next=so_shape, vel_next=vel_shape)
        following = []
        carried = {}
        for which in range(2):
            ins = dict(vel=vel, sh=sh, so=so, from_far=arrived[which][0], from_near=arrived[which][1],
                       **model, **carried)
            outs = dict(vel=vel_shape, **nexts)
            if step == 0 and which == 0:
                ins.update(model_near=model_near)
                outs.update(edges)
            scratch = []
            if final:
                first, last = plan.stress_tiles(step, which)
                scratch = [pltpu.VMEM((6, cx, (last - first) * ROWS, lanes), F32),
                           pltpu.SemaphoreType.DMA((3 * (1 - which) + 6 * len(plan.parts(first, last)),))]
            else:
                outs.update(sends(step + 1, which))
            got = call(functools.partial(advance, which=which), ins, outs, alias=("vel",) + tuple(carried) + (tuple(edges) if step + which == 0 else ()),
                       scratch=scratch, anywhere=("out",))
            vel = got["vel"]
            if step == 0 and which == 0:
                model.update({name: got[name] for name in edges})
            carried = {name: got[name] for name in nexts}
            if not final:
                following.append(exchange(got["send_far"], got["send_near"]))
        if final:
            return carried["out"]
        vel, sh, so, arrived = carried["vel_next"], carried["sh_next"], carried["so_next"], following


def cuts_of(steps, tiles):
    middle = tiles // 2 + 2
    return [max(1, middle - step) for step in range(steps)]


def solution(mesh):
    body = functools.partial(per_device, cuts_of, mesh.shape["shot"], mesh.shape["aper"])
    return jax.shard_map(
        body,
        mesh=mesh,
        in_specs=(
            P("shot", None, "aper", None, None),
            P("aper", "shot", None),
            P("aper", "shot", None),
            P("aper", "shot", None),
            P("aper", "shot", None),
            P(),
        ),
        out_specs=P("shot", None, "aper", None, None),
        check_vma=False,
    )
```

```python
import functools

import jax
import jax.numpy as jnp
from jax import lax
from jax.experimental import pallas as pl
from jax.experimental.pallas import tpu as pltpu
from jax.sharding import PartitionSpec as P

NEAR = 1.125
FAR = -1.0 / 24.0
RATIO = FAR / NEAR
DT = 0.2
ROWS = 8
PAD = 8
REACH = 3
VMEM = pl.BlockSpec(memory_space=pltpu.VMEM)
ANY = pl.BlockSpec(memory_space=pl.ANY)
F32 = jnp.float32


def call(body, ins, outs, alias=(), scratch=(), anywhere=(), us=5.0, waits=()):
    ins = dict(ins, **{"wait%d" % i: a for i, a in enumerate(waits)})
    in_names, out_names = list(ins), list(outs)

    def kernel(*refs):
        names = {}
        for name, ref in zip(in_names, refs):
            if name not in alias:
                names[name] = ref
        for name, ref in zip(out_names, refs[len(in_names):]):
            names[name] = ref
        body(names, *refs[len(in_names) + len(out_names):])

    ins = {name: pltpu.with_memory_space_constraint(a, pltpu.HBM) if name in anywhere
           else pltpu.with_memory_space_constraint(a, pltpu.VMEM) if name in alias
           else a for name, a in ins.items()}
    results = pl.pallas_call(
        kernel,
        out_shape=[pltpu.HBM(shape, F32) if name in anywhere else pltpu.VMEM(shape, F32)
                   for name, shape in outs.items()],
        in_specs=[ANY if name in anywhere or name[:4] == "wait" else VMEM for name in in_names],
        out_specs=[ANY if name in anywhere else VMEM for name in out_names],
        scratch_shapes=list(scratch),
        input_output_aliases={in_names.index(n): out_names.index(n) for n in alias},
        compiler_params=pltpu.CompilerParams(vmem_limit_bytes=24 * 2**20),
        cost_estimate=pl.CostEstimate(flops=int(us * 1e9), bytes_accessed=int(us * 3.6e6), transcendentals=0),
    )(*ins.values())
    return dict(zip(out_names, results))


def odd_slab():
    return lax.rem(lax.axis_index("aper"), 2) == 1


def pick(flag, yes, no):
    return jnp.where(flag, jnp.int32(yes), jnp.int32(no))


class Shifts:
    def __init__(self, lanes):
        lane = lax.broadcasted_iota(jnp.int32, (ROWS, lanes), 1)
        self.lanes = lanes
        self.f_up1 = jnp.where(lane < lanes - 1, F32(1), F32(0))
        self.f_up2 = jnp.where(lane < lanes - 2, F32(RATIO), F32(0))
        self.f_dn1 = jnp.where(lane >= 1, F32(RATIO), F32(0))
        self.b_dn1 = jnp.where(lane >= 1, F32(1), F32(0))
        self.b_dn2 = jnp.where(lane >= 2, F32(RATIO), F32(0))
        self.b_up1 = jnp.where(lane < lanes - 1, F32(RATIO), F32(0))

    def fz(self, f):
        n = self.lanes
        return (self.f_up1 * pltpu.roll(f, n - 1, 1) - f) + (
            self.f_up2 * pltpu.roll(f, n - 2, 1) - self.f_dn1 * pltpu.roll(f, 1, 1)
        )

    def bz(self, f):
        n = self.lanes
        return (f - self.b_dn1 * pltpu.roll(f, 1, 1)) + (
            self.b_up1 * pltpu.roll(f, n - 1, 1) - self.b_dn2 * pltpu.roll(f, 2, 1)
        )


def fwd(at):
    return (at(1) - at(0)) + RATIO * (at(2) - at(-1))


def bwd(at):
    return (at(0) - at(-1)) + RATIO * (at(1) - at(-2))


def tile_reader(ref, field, start):
    seen = {}

    def read(layer, dy=0):
        if (layer, dy) not in seen:
            seen[layer, dy] = ref[field, layer, pl.ds(start + PAD + dy, ROWS), :]
        return seen[layer, dy]

    return read


def factors(active_cells, damp):
    return jnp.where(active_cells, damp, F32(1)), jnp.where(active_cells, (DT * NEAR) * damp, F32(0))


def zero_pads(ref, rows):
    zeros = jnp.zeros((ref.shape[0], ref.shape[1], PAD, ref.shape[3]), F32)
    ref[:, :, :PAD, :] = zeros
    ref[:, :, PAD + rows:, :] = zeros


def zero_pad(ref, first):
    ref[:, :, first:first + PAD, :] = jnp.zeros((ref.shape[0], ref.shape[1], PAD, ref.shape[3]), F32)


class Plan:
    def __init__(self, cx, rows, lanes, blocks, steps, slabs, cuts):
        self.slabs = slabs
        self.cx, self.rows, self.lanes = cx, rows, lanes
        self.blocks, self.steps, self.cuts = blocks, steps, cuts
        self.block_rows = rows // blocks
        self.tiles = rows // ROWS

    def active(self, refs, moment, side, start):
        slab = jnp.clip(lax.axis_index("aper") + side - 1, 0, self.slabs - 1)
        row = (moment * self.slabs + slab) * self.blocks + start // self.block_rows
        return jnp.broadcast_to(refs["mask"][pl.ds(row, 1), :], (ROWS, self.lanes)) > 0

    def chunk(self, step, which):
        cut = self.cuts[step]
        return (0, cut) if which == 0 else (cut, self.tiles)

    def slots(self, step):
        n = self.cx
        if step < self.steps - 1:
            return [
                ((f, n + j), (f, REACH + j), (f, j), (f, n + REACH + j))
                for f in range(3) for j in range(REACH)
            ]
        top = [(0, n + 1), (0, n + 2), (1, n + 2), (2, n + 2), (2, n + 2)]
        bottom = [(0, 3), (1, 4), (1, 3), (2, 3), (2, 4)]
        below = [(0, 1), (0, 2), (1, 2), (2, 2), (2, 2)]
        above = [(0, n + 3), (1, n + 4), (1, n + 3), (2, n + 3), (2, n + 4)]
        return list(zip(top, bottom, below, above))

    def inner_forcing(self, refs, sh, so):
        z = Shifts(self.lanes)

        def tile(k, carry):
            start = pl.multiple_of(k * ROWS, ROWS)
            rows = pl.ds(start, ROWS)
            xy = tile_reader(sh, 1, start)
            xz = tile_reader(sh, 2, start)
            yy = tile_reader(so, 0, start)
            zz = tile_reader(so, 1, start)
            yz = tile_reader(so, 2, start)
            for i in range(self.cx):
                refs["inner"][0, i, rows, :] = bwd(lambda d: xy(i + 2, d)) + z.bz(xz(i + 2))
                refs["inner"][1, i, rows, :] = fwd(lambda d: yy(i, d)) + z.bz(yz(i))
                refs["inner"][2, i, rows, :] = bwd(lambda d: yz(i, d)) + z.fz(zz(i))
            return carry

        lax.fori_loop(0, self.tiles, tile, 0)

    def velocity(self, refs, moment, which, sh, so, previous):
        first, last = self.chunk(moment, which)
        z = Shifts(self.lanes)

        def tile(k, carry):
            start = pl.multiple_of(k * ROWS, ROWS)
            here = self.active(refs, moment, 1, start)
            xx = tile_reader(sh, 0, start)
            xy = tile_reader(sh, 1, start)
            xz = tile_reader(sh, 2, start)
            yy = tile_reader(so, 0, start)
            zz = tile_reader(so, 1, start)
            yz = tile_reader(so, 2, start)
            rows = pl.ds(start, ROWS)
            for i in range(self.cx):
                keep, gain = factors(here, refs["damp"][i, pl.ds(start, ROWS), :])
                gain = gain * refs["buoy"][i, pl.ds(start, ROWS), :]
                gx = fwd(lambda d: xx(i + 1 + d))
                gy = bwd(lambda d: xy(i + 2 + d))
                gz = bwd(lambda d: xz(i + 2 + d))
                if "inner" in refs:
                    gx = gx + refs["inner"][0, i, rows, :]
                    gy = gy + refs["inner"][1, i, rows, :]
                    gz = gz + refs["inner"][2, i, rows, :]
                else:
                    gx = gx + bwd(lambda d: xy(i + 2, d)) + z.bz(xz(i + 2))
                    gy = gy + fwd(lambda d: yy(i, d)) + z.bz(yz(i))
                    gz = gz + bwd(lambda d: yz(i, d)) + z.fz(zz(i))
                for f, g in enumerate((gx, gy, gz)):
                    refs["vel_next"][f, REACH + i, pl.ds(start + PAD, ROWS), :] = (
                        keep * previous(f, i, start) + gain * g
                    )
            return carry

        lax.fori_loop(first, last, tile, 0, unroll=True)
        odd = odd_slab()
        rows = pl.ds(PAD + first * ROWS, (last - first) * ROWS)
        for slot, (top, bottom, _, _) in enumerate(self.slots(moment)):
            field, layer = pick(odd, top[0], bottom[0]), pick(odd, top[1], bottom[1])
            refs["send_far"][slot] = refs["vel_next"][field, layer, rows, :]
            field, layer = pick(odd, bottom[0], top[0]), pick(odd, bottom[1], top[1])
            refs["send_near"][slot] = refs["vel_next"][field, layer, rows, :]

    def arrivals(self, refs, moment, which):
        first, last = self.chunk(moment, which)
        odd = odd_slab()
        rows = pl.ds(PAD + first * ROWS, (last - first) * ROWS)
        for slot, (_, _, below, above) in enumerate(self.slots(moment)):
            field, layer = pick(odd, above[0], below[0]), pick(odd, above[1], below[1])
            refs["vel"][field, layer, rows, :] = refs["from_far"][slot]
            field, layer = pick(odd, below[0], above[0]), pick(odd, below[1], above[1])
            refs["vel"][field, layer, rows, :] = refs["from_near"][slot]

    def stress_tiles(self, moment, which):
        first, last = self.chunk(moment, which)
        if which == 1:
            return first - 1, last
        return first, last - 1 if moment == self.steps - 1 else last

    def stress(self, refs, moment, which, final, part=None):
        first, last = part or self.stress_tiles(moment, which)
        base = self.stress_tiles(moment, which)[0]
        n = self.cx
        z = Shifts(self.lanes)
        old_h, old_o = refs["sh"], refs["so"]

        def tile(k, carry):
            start = pl.multiple_of(k * ROWS, ROWS)
            masks = [self.active(refs, moment, side, start) for side in range(3)]
            vx = tile_reader(refs["vel"], 0, start)
            vy = tile_reader(refs["vel"], 1, start)
            vz = tile_reader(refs["vel"], 2, start)
            rows = pl.ds(start, ROWS)
            padded = pl.ds(start + PAD, ROWS)

            def put_h(field, i, value):
                if final:
                    refs["done"][(0, 3, 4)[field], i, pl.ds(start - base * ROWS, ROWS), :] = value
                else:
                    refs["sh_next"][field, i + (1, 2, 2)[field], padded, :] = value

            def put_o(field, i, value):
                if final:
                    refs["done"][(1, 2, 5)[field], i, pl.ds(start - base * ROWS, ROWS), :] = value
                else:
                    refs["so_next"][field, i, padded, :] = value

            for i in range(0, n) if final else range(-2, n + 2):
                own = 0 <= i < n
                if own:
                    damp = refs["damp"][i, rows, :]
                else:
                    damp = refs["damp_edge"][i + 2 if i < 0 else i - n + 2, rows, :]
                keep, gain = factors(masks[0 if i < 0 else 1 if own else 2], damp)
                at = i + REACH
                mu = gain * refs["mu"][i + 2, rows, :]
                if i >= -1:
                    ex = bwd(lambda d: vx(at + d))
                    ey = bwd(lambda d: vy(at, d))
                    ez = z.bz(vz(at))
                    spread = gain * refs["lam"][i + 1, rows, :] * (ex + ey + ez)
                    mu2 = mu + mu
                    put_h(0, i, keep * old_h[0, i + 1, padded, :] + (spread + mu2 * ex))
                if own:
                    put_o(0, i, keep * old_o[0, i, padded, :] + (spread + mu2 * ey))
                    put_o(1, i, keep * old_o[1, i, padded, :] + (spread + mu2 * ez))
                    yz = z.fz(vy(at)) + fwd(lambda d: vz(at, d))
                    put_o(2, i, keep * old_o[2, i, padded, :] + mu * yz)
                if i <= n:
                    xy = fwd(lambda d: vx(at, d)) + fwd(lambda d: vy(at + d))
                    put_h(1, i, keep * old_h[1, i + 2, padded, :] + mu * xy)
                    xz = z.fz(vx(at)) + fwd(lambda d: vz(at + d))
                    put_h(2, i, keep * old_h[2, i + 2, padded, :] + mu * xz)
            return carry

        lax.fori_loop(first, last, tile, 0, unroll=True)

    def finish(self, refs, moment, which, done, sems):
        refs = dict(refs, done=done)
        first, last = self.stress_tiles(moment, which)
        copies = []

        def move(src, dst):
            copy = pltpu.make_async_copy(src, dst, sems.at[len(copies)])
            copy.start()
            copies.append(copy)

        if which == 0:
            for f in range(3):
                move(refs["vel"].at[f, pl.ds(REACH, self.cx), pl.ds(PAD, self.rows)], refs["out"].at[0, f])
        for a, b in self.parts(first, last):
            self.stress(refs, moment, which, True, (a, b))
            span = (b - a) * ROWS
            for f in range(6):
                move(done.at[f, :, pl.ds((a - first) * ROWS, span)],
                     refs["out"].at[0, 3 + f, :, pl.ds(a * ROWS, span)])
        for copy in copies:
            copy.wait()

    @staticmethod
    def parts(first, last):
        marks = [first, (first + last) // 2, last - (last - first) // 5, last]
        return [(a, b) for a, b in zip(marks, marks[1:]) if b > a]


STRESS_SLOTS = 5
MODEL_SLOTS = 6


def mover(sems):
    copies = []

    def move(src, dst):
        copy = pltpu.make_async_copy(src, dst, sems.at[len(copies)])
        copy.start()
        copies.append(copy)

    return move, copies


def pack_model(cx, refs, sems):
    odd = odd_slab()
    move, copies = mover(sems)
    for i, name in enumerate(("buoy", "q")):
        move(refs[name], refs["first"].at[pl.ds(i * cx, cx)])
    for i, name in enumerate(("lam", "mu", "q")):
        move(refs[name].at[pl.ds(pick(odd, cx - 2, 0), 2)], refs["edge"].at[pl.ds(2 * i, 2)])
    for i, name in enumerate(("lam", "mu")):
        move(refs[name], refs["second"].at[pl.ds(i * cx, cx)])
    for copy in copies:
        copy.wait()


def pack_stress(cx, refs, sems):
    odd = odd_slab()
    move, copies = mover(sems)
    top = [(3, cx - 1), (6, cx - 2), (6, cx - 1), (7, cx - 2), (7, cx - 1)]
    bottom = [(3, 0), (3, 1), (6, 0), (7, 0), (7, 0)]
    for name, flag in (("near", jnp.logical_not(odd)), ("far", odd)):
        for slot in range(STRESS_SLOTS):
            field = pick(flag, top[slot][0], bottom[slot][0])
            layer = pick(flag, top[slot][1], bottom[slot][1])
            move(refs["wave"].at[0, field, layer], refs[name].at[slot])
    for copy in copies:
        copy.wait()


def prepare(plan, refs):
    cx, rows = plan.cx, plan.rows
    zero_pads(refs["sh"], rows)
    zero_pads(refs["so"], rows)
    inner = pl.ds(PAD, rows)
    for field, (source, shift) in enumerate(((3, 1), (6, 2), (7, 2))):
        for i in range(cx):
            refs["sh"][field, i + shift, inner, :] = refs["wave"][0, source, i]
    for field, source in enumerate((4, 5, 8)):
        for i in range(cx):
            refs["so"][field, i, inner, :] = refs["wave"][0, source, i]
    for field in range(3):
        for i in range(cx):
            refs["old"][field, i] = refs["wave"][0, field, i]
    plan.inner_forcing(refs, refs["sh"], refs["so"])
    lane_blocks = refs["active"].shape[1]
    block = lax.broadcasted_iota(jnp.int32, (lane_blocks, plan.lanes), 1) // (plan.lanes // lane_blocks)
    own = block == lax.broadcasted_iota(jnp.int32, (lane_blocks, plan.lanes), 0)
    refs["mask"][...] = jnp.dot(refs["active"][...].astype(F32), own.astype(F32),
                                preferred_element_type=F32)


def hold(array, *others):
    return call(lambda refs: None, dict(array=array), dict(array=array.shape), alias=("array",),
                us=0.02, waits=others)["array"]


def spread(mine, shots):
    pairs = lambda k: [(i, i ^ k) for i in range(shots)]
    if shots == 4:
        beside = lax.ppermute(mine, "shot", pairs(1))
        across = lax.ppermute(mine, "shot", pairs(2))

        def finish(*others):
            held = hold(across, beside, *others)
            handed = lax.ppermute(held, "shot", pairs(1))
            return {0: mine, 1: beside, 2: across, 3: handed}, held

        return (beside, across), finish
    turn = lambda k: [(i, (i + k) % shots) for i in range(shots)]
    swap = shots & (shots - 1) == 0
    got = {k: lax.ppermute(mine, "shot", pairs(k) if swap else turn(k)) for k in range(1, shots)}
    return tuple(got.values()), lambda *others: ({0: mine, **got}, mine)


def origin_of(index, k, shots):
    if shots & (shots - 1) == 0:
        return index ^ k
    return lax.rem(index + shots - k, shots)


def panel_place(k, shots, panel_rows):
    start = origin_of(lax.axis_index("shot"), k, shots) * panel_rows
    return pl.ds(pl.multiple_of(start, panel_rows), panel_rows)


def per_device(cuts_of, shots, slabs, wave, lam, mu, buoy, q, active):
    cx, panel_rows, lanes = lam.shape
    rows = wave.shape[3]
    steps, _, blocks, lane_blocks = active.shape
    plan = Plan(cx, rows, lanes, blocks, steps, slabs, cuts_of(steps, rows // ROWS))
    padded = rows + 2 * PAD
    far = [(i, i + 1) for i in range(1, slabs - 1, 2)]
    near = [(i, i + 1) for i in range(0, slabs - 1, 2)]
    far = far + [(j, i) for i, j in far]
    near = near + [(j, i) for i, j in near]

    def exchange(to_far, to_near):
        return lax.ppermute(to_far, "aper", far), lax.ppermute(to_near, "aper", near)

    panel = (panel_rows, lanes)
    sent = call(
        functools.partial(pack_model, cx), dict(lam=lam, mu=mu, buoy=buoy, q=q),
        dict(first=(2 * cx,) + panel, second=(2 * cx,) + panel, edge=(MODEL_SLOTS,) + panel),
        scratch=[pltpu.SemaphoreType.DMA((7,))], anywhere=("lam", "mu", "buoy", "q"), us=0.02,
    )
    edge = lax.ppermute(sent["edge"], "aper", far)
    sent.update(call(
        functools.partial(pack_stress, cx), dict(wave=wave),
        dict(far=(STRESS_SLOTS, rows, lanes), near=(STRESS_SLOTS, rows, lanes)),
        scratch=[pltpu.SemaphoreType.DMA((2 * STRESS_SLOTS,))], anywhere=("wave",), us=5.0, waits=(edge,),
    ))
    halo_far, halo_near = exchange(sent["far"], sent["near"])
    sh_shape, so_shape = (3, cx + 3, padded, lanes), (3, cx, padded, lanes)
    vel_shape, slab_shape = (3, cx + 2 * REACH, padded, lanes), (cx, rows, lanes)
    state = call(functools.partial(prepare, plan), dict(wave=wave, active=active.reshape(-1, lane_blocks)),
                 dict(sh=sh_shape, so=so_shape, old=(3,) + slab_shape, inner=(3,) + slab_shape, mask=(steps * slabs * blocks, lanes)), us=5.0)

    first_stage, finish = spread(sent["first"], shots)
    mask = state["mask"]
    firsts, held = finish(edge)

    def mark(refs):
        refs["tick"][...] = jnp.zeros(refs["tick"].shape, F32)

    tick = call(mark, {}, dict(tick=(ROWS, lanes)), waits=(held,))["tick"]

    def join(refs):
        refs["all"][:2 * cx] = refs["second"][...]
        refs["all"][2 * cx:] = refs["edge"][...]

    second = call(join, dict(second=sent["second"], edge=edge),
                  dict(all=(2 * cx + MODEL_SLOTS,) + panel), us=0.02, waits=first_stage + (tick,))["all"]
    _, finish_second = spread(second, shots)

    def sends(step, which):
        first, last = plan.chunk(step, which)
        shape = (len(plan.slots(step)), (last - first) * ROWS, lanes)
        return dict(send_far=shape, send_near=shape)

    def start_first(refs):
        odd = odd_slab()
        inner = pl.ds(PAD, rows)
        below = [(0, 0), (1, 0), (1, 1), (2, 0), (2, 1)]
        above = [(0, cx + 1), (0, cx + 2), (1, cx + 2), (2, cx + 2), (2, cx + 2)]
        for slot in range(STRESS_SLOTS):
            field = pick(odd, above[slot][0], below[slot][0])
            layer = pick(odd, above[slot][1], below[slot][1])
            refs["sh"][field, layer, inner, :] = refs["halo_far"][slot]
            field = pick(odd, below[slot][0], above[slot][0])
            layer = pick(odd, below[slot][1], above[slot][1])
            refs["sh"][field, layer, inner, :] = refs["halo_near"][slot]
        for k in firsts:
            place, got = panel_place(k, shots, panel_rows), refs["first%d" % k]
            for i in range(cx):
                refs["buoy"][i, place, :] = got[i]
                refs["damp"][i, place, :] = jnp.exp(-DT * got[cx + i])
        zero_pads(refs["vel_next"], rows)
        start_chunk(refs, 0)

    def start_chunk(refs, which):
        plan.velocity(refs, 0, which, refs["sh"], refs["so"],
                      lambda f, i, start: refs["old"][f, i, pl.ds(start, ROWS), :])

    ins = dict(halo_far=halo_far, halo_near=halo_near, **state)
    ins.update({"first%d" % k: a for k, a in firsts.items()})
    got = call(start_first, ins,
               dict(sh=sh_shape, buoy=slab_shape, damp=slab_shape, vel_next=vel_shape,
                    **sends(0, 0)),
               alias=("sh",), us=1.2)
    sh, so = got["sh"], state["so"]
    model = dict(mask=mask, buoy=got["buoy"], damp=got["damp"])
    arrived = [exchange(got["send_far"], got["send_near"])]
    got = call(lambda refs: start_chunk(refs, 1),
               dict(sh=sh, so=so, old=state["old"], inner=state["inner"], vel_next=got["vel_next"], **model),
               dict(vel_next=vel_shape, **sends(0, 1)), alias=("vel_next",), us=0.8)
    vel = got["vel_next"]
    arrived.append(exchange(got["send_far"], got["send_near"]))

    seconds, _ = finish_second()

    def put_edge(refs, from_above, place, part):
        for j in range(2):
            refs["lam"][pick(from_above, cx + 1 + j, 0), place, :] = part(j)
            refs["mu"][pick(from_above, cx + 2 + j, j), place, :] = part(2 + j)
            refs["damp_edge"][pick(from_above, 2 + j, j), place, :] = part(4 + j)

    def assemble(refs):
        odd = odd_slab()
        for k in seconds:
            place, got = panel_place(k, shots, panel_rows), refs["second%d" % k]
            for i in range(cx):
                refs["lam"][i + 1, place, :] = got[i]
                refs["mu"][i + 2, place, :] = got[cx + i]
            put_edge(refs, odd, place, lambda slot: jnp.exp(-DT * got[2 * cx + slot])
                     if slot >= 4 else got[2 * cx + slot])
        for j in range(2):
            at = pick(odd, j, cx - 2 + j)
            refs["send_model"][j] = refs["lam"][at + 1]
            refs["send_model"][2 + j] = refs["mu"][at + 2]
            refs["send_model"][4 + j] = refs["damp"][at]

    edges = dict(lam=(cx + 3, rows, lanes), mu=(cx + 4, rows, lanes), damp_edge=(4, rows, lanes))
    got = call(assemble, dict(damp=model["damp"], **{"second%d" % k: a for k, a in seconds.items()}),
               dict(send_model=(MODEL_SLOTS, rows, lanes), **edges), us=0.02, waits=(arrived[1][1],))
    model_near = lax.ppermute(got["send_model"], "aper", near)
    model.update({name: got[name] for name in edges})
    vel = call(lambda refs: plan.arrivals(refs, 0, 0),
               dict(vel=vel, from_far=arrived[0][0], from_near=arrived[0][1]),
               dict(vel=vel_shape), alias=("vel",), us=20.0)["vel"]

    out_shape = wave.shape
    for step in range(steps):
        final = step == steps - 1

        def advance(refs, *scratch, which, step=step, final=final):
            if step == 0 and which == 0:
                put_edge(refs, jnp.logical_not(odd_slab()), slice(None), lambda slot: refs["model_near"][slot])
            else:
                plan.arrivals(refs, step, which)
            if final:
                plan.finish(refs, step, which, *scratch)
                return
            for name in ("sh_next", "so_next", "vel_next"):
                zero_pad(refs[name], 0 if which == 0 else PAD + rows)
            plan.stress(refs, step, which, False)
            plan.velocity(
                refs, step + 1, which, refs["sh_next"], refs["so_next"],
                lambda f, i, start: refs["vel"][f, REACH + i, pl.ds(start + PAD, ROWS), :])

        nexts = dict(out=out_shape) if final else dict(
            sh_next=sh_shape, so_next=so_shape, vel_next=vel_shape)
        following = []
        carried = {}
        for which in range(2):
            ins = dict(vel=vel, sh=sh, so=so, from_far=arrived[which][0], from_near=arrived[which][1],
                       **model, **carried)
            outs = dict(vel=vel_shape, **nexts)
            if step == 0 and which == 0:
                ins.update(model_near=model_near)
                outs.update(edges)
            scratch = []
            if final:
                first, last = plan.stress_tiles(step, which)
                scratch = [pltpu.VMEM((6, cx, (last - first) * ROWS, lanes), F32),
                           pltpu.SemaphoreType.DMA((3 * (1 - which) + 6 * len(plan.parts(first, last)),))]
            else:
                outs.update(sends(step + 1, which))
            got = call(functools.partial(advance, which=which), ins, outs, alias=("vel",) + tuple(carried) + (tuple(edges) if step + which == 0 else ()),
                       scratch=scratch, anywhere=("out",))
            vel = got["vel"]
            if step == 0 and which == 0:
                model.update({name: got[name] for name in edges})
            carried = {name: got[name] for name in nexts}
            if not final:
                following.append(exchange(got["send_far"], got["send_near"]))
        if final:
            return carried["out"]
        vel, sh, so, arrived = carried["vel_next"], carried["sh_next"], carried["so_next"], following


def cuts_of(steps, tiles):
    middle = tiles // 2 + 2
    return [max(1, middle - step) for step in range(steps)]


def solution(mesh):
    body = functools.partial(per_device, cuts_of, mesh.shape["shot"], mesh.shape["aper"])
    return jax.shard_map(
        body,
        mesh=mesh,
        in_specs=(
            P("shot", None, "aper", None, None),
            P("aper", "shot", None),
            P("aper", "shot", None),
            P("aper", "shot", None),
            P("aper", "shot", None),
            P(),
        ),
        out_specs=P("shot", None, "aper", None, None),
        check_vma=False,
    )
```
